256 devices in a mesh: ta: 8 (over z_lo, core), xyz: 32 (over x, y, z_hi).
Axes of the slice: x: 4, y: 4, z: 8 (z_hi: 2, z_lo: 4; z = z_hi * 4 + z_lo), core: 2. Of those that a mesh axis runs over, the one named last changes fastest.
Arguments:
- fine_field: bfloat16 [8, 128, 32, 6144], P('ta', 'xyz'), may hold values from -6 to 6
- null_vectors: bfloat16 [8, 128, 96, 6144], P('ta', 'xyz'), may hold values from -0.21875 to 0.21875
- coarse_blocks: bfloat16 [8, 128, 9, 9216], P('ta', 'xyz'), may hold values from -0.125 to 0.125
- neighbours: int32 [128, 6], replicated, may hold values from 0 to 127, as said below
- owner_map: int32 [128], replicated, may hold values from 0 to 127, as said below
Outputs:
- correction: bfloat16 [8, 128, 32, 6144], P('ta', 'xyz')
The draws below stay inside these ranges and needn't reach their ends.
Inputs may be any that keep to these rules, and one draw needn't show every extreme that they name: Each row names six different coarse positions, the spatial neighbours of a position on a periodic lattice. The groups of four positions (4 k to 4 k + 3) form a periodic grid of 8 rows of four groups: group k lies in row k // 4 at slot k % 4. The +x and -x neighbours of a position lie in the groups of its own row whose slots follow and precede its group's slot on the cycle 0, 2, 1, 3, 0; its +y and -y neighbours lie in the groups 4 places above and below, cyclically over the 32 groups; its +z and -z neighbours lie in its own group. Each group orders its four positions as a cycle along z, in an order of its own; the x and y neighbours of a position hold the same place on their group's cycle as the position on its own. `owner_map`: A permutation of the coarse positions. The four aggregates 4 d to 4 d + 3 of the fine order go to the positions d + s * (32) for s = 0, 1, 2, 3, one each, in some order.
All inputs are finite; a program needn't handle non-finite values.
Results may differ from the reference program's by a relative error of at most 0.0085.
Values may be sent and summed in bfloat16 or wider, within the bound.
A program may use at most 64 MiB of HBM per device.

```python
import jax
import jax.numpy as jnp
from jax import lax

KF = 6144
NC = 96
NRHS = 32
APPLIES = 3
SITES = 128
SLABS = 8


def draw_neighbours(key, part):
    key = jax.random.fold_in(key, 7)
    groups = SITES // 4
    rows = groups // 4
    group_keys = jax.random.split(key, groups)
    slot_order = jax.vmap(lambda single: jax.random.permutation(single, 4))(group_keys).astype(jnp.int32)
    inverse = jnp.argsort(slot_order, axis=1).astype(jnp.int32)
    base_order = jnp.array([0, 2, 1, 3], dtype=jnp.int32)
    position = jnp.arange(SITES, dtype=jnp.int32)
    group = position // 4
    row_index = group // 4
    column_index = group % 4
    depth = inverse[group, position % 4]
    across = base_order[column_index]

    def locate(across_value, row_value, depth_value):
        wrapped_row = jnp.mod(row_value, rows)
        target_group = wrapped_row * 4 + base_order[jnp.mod(across_value, 4)]
        return target_group * 4 + slot_order[target_group, jnp.mod(depth_value, 4)]
    columns = [locate(across + 1, row_index, depth), locate(across - 1, row_index, depth), locate(across, row_index + 1, depth), locate(across, row_index - 1, depth), locate(across, row_index, depth + 1), locate(across, row_index, depth - 1)]
    return jnp.stack(columns, axis=1).astype(jnp.int32)


def draw_owner_map(key, part):
    key = jax.random.fold_in(key, 11)
    groups = SITES // 4
    group_keys = jax.random.split(key, groups)
    spread = jax.vmap(lambda single: jax.random.permutation(single, 4))(group_keys).astype(jnp.int32)
    source_group = jnp.arange(SITES, dtype=jnp.int32) // 4
    return (source_group + spread.reshape(-1) * groups).astype(jnp.int32)


def block_levels(rng, extent, cuts, low, high):
    level = 1.0
    for dim, shards_of in cuts:
        draws = jax.random.uniform(jax.random.fold_in(jax.random.fold_in(rng, 6), dim), (shards_of,), jnp.float32, low / len(cuts), high / len(cuts))
        level = level * jnp.repeat(jnp.exp(draws), extent[dim] // shards_of).reshape((-1,) + (1,) * (len(extent) - 1 - dim))
    return level


def bell_draw(stream_key, shape, deviation, reach, shards=(), held_as=jnp.bfloat16):
    entries = jax.random.normal(stream_key, shape, jnp.float32) * deviation
    if len(shards) > 0:
        entries = block_levels(stream_key, shape, shards, -0.22, 0.18) * entries
    return jnp.clip(entries, min=-reach, max=reach).astype(held_as)


def setup_inputs(seed: int = 0) -> dict:
    seeds = jax.random.split(jax.random.key(seed), 6)
    fine_field = bell_draw(seeds[0], (SLABS, SITES, NRHS, KF), 1.0, 6.0, ((0, 8), (1, 32)))
    null_vectors = bell_draw(seeds[1], (SLABS, SITES, NC, KF), (8 * NC) ** -0.5, 0.21875, ((0, 8), (1, 32)))
    coarse_blocks = bell_draw(seeds[2], (SLABS, SITES, 9, NC * NC), (27 * NC) ** -0.5, 0.125, ((0, 8), (1, 32)))
    neighbours = draw_neighbours(jax.random.fold_in(seeds[5], 71), 0)
    owner_map = draw_owner_map(jax.random.fold_in(seeds[5], 71), 0)
    return dict(fine_field=fine_field, null_vectors=null_vectors, coarse_blocks=coarse_blocks, neighbours=neighbours, owner_map=owner_map)


def restrict_slab(slab_pair):
    spinor, vectors = slab_pair
    return jnp.einsum("abk,ack->abc", spinor.astype(jnp.float32), vectors.astype(jnp.float32))


def prolong_slab(slab_pair):
    coarse, vectors = slab_pair
    return jnp.einsum("abc,ack->abk", coarse.astype(jnp.float32), vectors.astype(jnp.float32))


def reference(fine_field, null_vectors, coarse_blocks, neighbours, owner_map):
    restricted = lax.map(restrict_slab, (fine_field, null_vectors)).astype(jnp.bfloat16)
    right_side = jnp.zeros_like(restricted).at[:, owner_map].set(restricted)
    blocks = coarse_blocks.reshape(SLABS, SITES, 9, NC, NC).astype(jnp.float32)

    def apply_operator(spinor):
        gathered = [spinor] + [spinor[:, neighbours[:, column]] for column in range(6)]
        gathered = gathered + [jnp.roll(spinor, -1, axis=0), jnp.roll(spinor, 1, axis=0)]
        stacked = jnp.stack(gathered, axis=2).astype(jnp.float32)
        return jnp.einsum("tsmcn,tsmbn->tsbc", blocks, stacked)

    solution = right_side
    for sweep in range(APPLIES):
        solution = (right_side.astype(jnp.float32) - apply_operator(solution)).astype(jnp.bfloat16)
    back = solution[:, owner_map]
    return lax.map(prolong_slab, (back, null_vectors)).astype(jnp.bfloat16)
```

```python
import jax
import jax.numpy as jnp
from jax import lax
from jax.experimental import pallas as pl
from jax.experimental.pallas import tpu as pltpu
from jax.sharding import PartitionSpec as P

MESH = pl.DeviceIdType.MESH
APPLIES = 3
SITES = 4
NRHS = 32
NC = 96
LANES = 128
KF = 6144
CUTS = 2
PIECE = KF // CUTS
OUT_PIECE = 1024
NT = (((1,), (1,)), ((), ()))


def dot_nt(a, b):
    return lax.dot_general(a, b, NT, preferred_element_type=jnp.float32)


def kernel(
    fine_hbm, null_hbm, blocks_hbm, neighbours, owner_map, out_hbm,
    fine, null, blocks, weights, out, rest, outgoing, rhs, fields, halos, returned,
    load_sem, block_sem, out_sem, go_send, go_recv, halo_send, halo_recv, back_send, back_recv,
):
    t = lax.axis_index("ta")
    d = lax.axis_index("xyz")

    dests = [d // 4 + 8 * s for s in range(4)]
    sources = [4 * (d % 8) + j for j in range(4)]
    slot = d % 4
    across = (slot % 2) * 2 + slot // 2
    after, before = (across + 1) % 4, (across + 3) % 4
    row = d - slot
    x_up = row + (after % 2) * 2 + after // 2
    x_down = row + (before % 2) * 2 + before // 2
    y_up, y_down = (d + 4) % 32, (d + 28) % 32
    t_up, t_down = (t + 1) % 8, (t + 7) % 8
    sides = [
        ((t, x_down), 1), ((t, x_up), 2),
        ((t, y_down), 3), ((t, y_up), 4),
        ((t_down, d), 7), ((t_up, d), 8),
    ]

    loads = []
    for a in range(SITES):
        for c in range(CUTS):
            part = pl.ds(c * PIECE, PIECE)
            pair = [
                pltpu.make_async_copy(
                    fine_hbm.at[a, :, part], fine.at[a, :, part], load_sem.at[0, a * CUTS + c]
                ),
                pltpu.make_async_copy(
                    null_hbm.at[a, :, part], null.at[a, :, part], load_sem.at[1, a * CUTS + c]
                ),
            ]
            for copy in pair:
                copy.start()
            loads.append(pair)
    load_blocks = pltpu.make_async_copy(blocks_hbm, blocks, block_sem)
    load_blocks.start()

    barrier = pltpu.get_barrier_semaphore()
    for (to_t, to_d), _ in sides:
        pl.semaphore_signal(barrier, inc=1, device_id=(to_t, to_d), device_id_type=MESH)
    for partner in dests + sources:
        @pl.when(partner != d)
        def _():
            pl.semaphore_signal(barrier, inc=1, device_id=(t, partner), device_id_type=MESH)

    for ref in [rest] + list(fields):
        ref[...] = jnp.zeros_like(ref)
    weights[...] = jnp.zeros_like(weights)

    for a in range(SITES):
        total = jnp.zeros((NRHS, NC), jnp.float32)
        for c in range(CUTS):
            for copy in loads[a * CUTS + c]:
                copy.wait()
            part = pl.ds(c * PIECE, PIECE)
            total += dot_nt(fine[a, :, part], null[a, :, part])
        rest[a, :, :NC] = total.astype(jnp.bfloat16)

    strides = [owner_map[4 * d + a] // 32 for a in range(SITES)]
    for s in range(4):
        chosen = 0
        for a in range(1, SITES):
            chosen = jnp.where(strides[a] == s, a, chosen)
        outgoing[s] = rest[chosen]

    own = 0
    for partner in dests:
        own = own + jnp.where(partner == d, 1, 0)
    pl.semaphore_wait(barrier, 6 + 8 - 2 * own)

    def go(s):
        return pltpu.make_async_remote_copy(
            src_ref=outgoing.at[s], dst_ref=rhs.at[slot],
            send_sem=go_send.at[s], recv_sem=go_recv.at[slot],
            device_id=(t, dests[s]), device_id_type=MESH,
        )

    def arrived(j):
        return pltpu.make_async_remote_copy(
            src_ref=outgoing.at[j], dst_ref=rhs.at[j],
            send_sem=go_send.at[j], recv_sem=go_recv.at[j],
            device_id=(t, d), device_id_type=MESH,
        )

    for s in range(4):
        @pl.when(dests[s] != d)
        def _():
            go(s).start()

        @pl.when(dests[s] == d)
        def _():
            rhs[slot] = outgoing[s]

    load_blocks.wait()
    for s in range(SITES):
        for m in range(9):
            weights[s, :, m * LANES : m * LANES + NC] = blocks[m, s]

    for j in range(4):
        @pl.when(sources[j] != d)
        def _():
            arrived(j).wait_recv()

    places = [[neighbours[c, 4 * d + s] % 4 for c in range(6)] for s in range(SITES)]
    for k in range(APPLIES):
        field = rhs if k == 0 else fields[k - 1]
        copies = {}
        for i, ((to_t, to_d), m) in enumerate(sides):
            copies[m] = pltpu.make_async_remote_copy(
                src_ref=field, dst_ref=halos[6 * k + i],
                send_sem=halo_send.at[k, i], recv_sem=halo_recv.at[k, i],
                device_id=(to_t, to_d), device_id_type=MESH,
            )
            copies[m].start()

        def piece(s, ms, inputs):
            total = None
            for m, x in zip(ms, inputs):
                term = dot_nt(x, weights[s, :, m * LANES : (m + 1) * LANES])
                total = term if total is None else total + term
            return total

        totals = [
            piece(s, (0, 5, 6), (field[s], field[places[s][4]], field[places[s][5]]))
            for s in range(SITES)
        ]
        for ms in ((7, 8), (3, 4), (1, 2)):
            for m in ms:
                copies[m].wait_recv()
            first = halos[6 * k + [side[1] for side in sides].index(ms[0])]
            second = halos[6 * k + [side[1] for side in sides].index(ms[1])]
            for s in range(SITES):
                if ms[0] == 7:
                    pair = (first[s], second[s])
                else:
                    pair = (first[places[s][ms[0] - 1]], second[places[s][ms[1] - 1]])
                totals[s] = totals[s] + piece(s, ms, pair)
        for s in range(SITES):
            new = rhs[s, :, :NC].astype(jnp.float32) - totals[s]
            fields[k][s, :, :NC] = new.astype(jnp.bfloat16)
        for copy in copies.values():
            copy.wait_send()

    answer = fields[APPLIES - 1]
    stride = d // 8

    def come(j):
        return pltpu.make_async_remote_copy(
            src_ref=answer.at[j], dst_ref=returned.at[stride],
            send_sem=back_send.at[j], recv_sem=back_recv.at[stride],
            device_id=(t, sources[j]), device_id_type=MESH,
        )

    def came(s):
        return pltpu.make_async_remote_copy(
            src_ref=answer.at[s], dst_ref=returned.at[s],
            send_sem=back_send.at[s], recv_sem=back_recv.at[s],
            device_id=(t, d), device_id_type=MESH,
        )

    for j in range(4):
        @pl.when(sources[j] != d)
        def _():
            come(j).start()

        @pl.when(sources[j] == d)
        def _():
            returned[stride] = answer[j]
    for s in range(4):
        @pl.when(dests[s] != d)
        def _():
            go(s).wait_send()
            came(s).wait_recv()

    stores = []
    for a in range(SITES):
        back = returned[strides[a]][:, :NC]
        for c in range(KF // OUT_PIECE):
            part = pl.ds(c * OUT_PIECE, OUT_PIECE)
            out[a, :, part] = jnp.dot(
                back, null[a, :, part], preferred_element_type=jnp.float32
            ).astype(jnp.bfloat16)
        copy = pltpu.make_async_copy(out.at[a], out_hbm.at[a], out_sem.at[a])
        copy.start()
        stores.append(copy)
    for j in range(4):
        @pl.when(sources[j] != d)
        def _():
            come(j).wait_send()
    for copy in stores:
        copy.wait()


def body(fine_field, null_vectors, coarse_blocks, neighbours, owner_map):
    blocks = coarse_blocks.reshape(SITES, 9, NC, NC).transpose(1, 0, 2, 3)
    hbm = pl.BlockSpec(memory_space=pl.ANY)
    smem = pl.BlockSpec(memory_space=pltpu.SMEM)
    field = pltpu.VMEM((SITES, NRHS, LANES), jnp.bfloat16)
    dma = pltpu.SemaphoreType.DMA
    result = pl.pallas_call(
        kernel,
        out_shape=jax.ShapeDtypeStruct((SITES, NRHS, KF), jnp.bfloat16),
        in_specs=[hbm, hbm, hbm, smem, smem],
        out_specs=hbm,
        scratch_shapes=[
            pltpu.VMEM((SITES, NRHS, KF), jnp.bfloat16),
            pltpu.VMEM((SITES, NC, KF), jnp.bfloat16),
            pltpu.VMEM((9, SITES, NC, NC), jnp.bfloat16),
            pltpu.VMEM((SITES, NC, 9 * LANES), jnp.bfloat16),
            pltpu.VMEM((SITES, NRHS, KF), jnp.bfloat16),
            field, field, field,
            [field] * APPLIES,
            [field] * (6 * APPLIES),
            field,
            dma((2, SITES * CUTS)), dma, dma((SITES,)),
            dma((4,)), dma((4,)),
            dma((APPLIES, 6)), dma((APPLIES, 6)),
            dma((4,)), dma((4,)),
        ],
        compiler_params=pltpu.CompilerParams(
            collective_id=0, has_side_effects=True, vmem_limit_bytes=40 * 1024 * 1024
        ),
    )(fine_field[0], null_vectors[0], blocks, neighbours.T, owner_map)
    return result[None]


def solution(mesh):
    in_specs = (
        P("ta", "xyz", None, None),
        P("ta", "xyz", None, None),
        P("ta", "xyz", None, None),
        P(),
        P(),
    )
    out_specs = P("ta", "xyz", None, None)
    return jax.shard_map(body, mesh=mesh, in_specs=in_specs, out_specs=out_specs, check_vma=False)
```

```python
import jax
import jax.numpy as jnp
from jax import lax
from jax.experimental import pallas as pl
from jax.experimental.pallas import tpu as pltpu
from jax.sharding import PartitionSpec as P

MESH = pl.DeviceIdType.MESH
APPLIES = 3
SITES = 4
NRHS = 32
NC = 96
LANES = 128
KF = 6144
CUTS = 2
PIECE = KF // CUTS
OUT_PIECE = 2048
NT = (((1,), (1,)), ((), ()))


def dot_nt(a, b):
    return lax.dot_general(a, b, NT, preferred_element_type=jnp.float32)


def kernel(
    fine_hbm, null_hbm, blocks_hbm, neighbours_hbm, owner_hbm, null, back,
    fine, raw, spread, square, weights, neighbours, owner_map,
    rest, outgoing, rhs, fields, halos, returned,
    load_sem, table_sem, go_send, go_recv, halo_send, halo_recv, back_send, back_recv,
):
    t = lax.axis_index("ta")
    d = lax.axis_index("xyz")

    dests = [d // 4 + 8 * s for s in range(4)]
    sources = [4 * (d % 8) + j for j in range(4)]
    slot = d % 4
    across = (slot % 2) * 2 + slot // 2
    odd = across % 2
    far_at, near_at = (across + 3 + 2 * odd) % 4, (across + 1 + 2 * odd) % 4
    far = d - slot + (far_at % 2) * 2 + far_at // 2
    near = d - slot + (near_at % 2) * 2 + near_at // 2
    far_m, near_m = 2 - odd, 1 + odd
    y_up, y_down = (d + 4) % 32, (d + 28) % 32
    t_up, t_down = (t + 1) % 8, (t + 7) % 8
    sides = [
        ((t, far), far_m), ((t, near), near_m),
        ((t, y_down), 3), ((t, y_up), 4),
        ((t_down, d), 7), ((t_up, d), 8),
    ]

    barrier = pltpu.get_barrier_semaphore()
    for partner in sources + dests:
        @pl.when(partner != d)
        def _():
            pl.semaphore_signal(barrier, inc=1, device_id=(t, partner), device_id_type=MESH)
    for (to_t, to_d), _ in sides:
        pl.semaphore_signal(barrier, inc=1, device_id=(to_t, to_d), device_id_type=MESH)

    loads = []
    for a in range(SITES):
        for c in range(CUTS):
            part = pl.ds(c * PIECE, PIECE)
            pair = [
                pltpu.make_async_copy(
                    fine_hbm.at[a, :, part], fine.at[a, :, part], load_sem.at[0, a * CUTS + c]
                ),
                pltpu.make_async_copy(
                    null_hbm.at[a, :, part], null.at[a, :, part], load_sem.at[1, a * CUTS + c]
                ),
            ]
            for copy in pair:
                copy.start()
            loads.append(pair)
    load_tables = [
        pltpu.make_async_copy(owner_hbm, owner_map, table_sem.at[0]),
        pltpu.make_async_copy(neighbours_hbm, neighbours, table_sem.at[1]),
        pltpu.make_async_copy(blocks_hbm, raw, table_sem.at[2]),
    ]
    for copy in load_tables:
        copy.start()

    for ref in [rest] + list(fields):
        ref[...] = jnp.zeros_like(ref)

    for a in range(SITES):
        total = jnp.zeros((NRHS, NC), jnp.float32)
        for c in range(CUTS):
            for copy in loads[a * CUTS + c]:
                copy.wait()
            part = pl.ds(c * PIECE, PIECE)
            total += dot_nt(fine[a, :, part], null[a, :, part])
        rest[a, :, :NC] = total.astype(jnp.bfloat16)

    load_tables[0].wait()
    load_tables[1].wait()
    strides = [owner_map[4 * d + a] // 32 for a in range(SITES)]
    for s in range(4):
        chosen = 0
        for a in range(1, SITES):
            chosen = jnp.where(strides[a] == s, a, chosen)
        outgoing[s] = rest[chosen]

    own = 0
    for partner in dests:
        own = own + jnp.where(partner == d, 1, 0)
    pl.semaphore_wait(barrier, 6 + 8 - 2 * own)

    def go(s):
        return pltpu.make_async_remote_copy(
            src_ref=outgoing.at[s], dst_ref=rhs.at[slot],
            send_sem=go_send.at[s], recv_sem=go_recv.at[slot],
            device_id=(t, dests[s]), device_id_type=MESH,
        )

    def arrived(j):
        return pltpu.make_async_remote_copy(
            src_ref=outgoing.at[j], dst_ref=rhs.at[j],
            send_sem=go_send.at[j], recv_sem=go_recv.at[j],
            device_id=(t, d), device_id_type=MESH,
        )

    for s in range(4):
        @pl.when(dests[s] != d)
        def _():
            go(s).start()

        @pl.when(dests[s] == d)
        def _():
            rhs[slot] = outgoing[s]

    def product(s, ms, inputs):
        matrices = [weights[m, s] for m in ms]
        return dot_nt(jnp.concatenate(inputs, axis=1), jnp.concatenate(matrices, axis=1))

    load_tables[2].wait()
    lane = lax.broadcasted_iota(jnp.int32, (NC // 4, LANES), 1)

    @pl.loop(0, 9)
    def _(m):
        for j in range(72):
            spread[m, 8 * j : 8 * j + SITES, :] = raw[m, :, j * LANES : (j + 1) * LANES].astype(
                jnp.float32
            )
        for s in range(SITES):
            f0, f1, f2 = [spread[m, pl.ds(8 * j + s, NC // 4, stride=24), :] for j in range(3)]
            rows = [
                f0,
                jnp.where(lane < 32, pltpu.roll(f0, 32, 1), pltpu.roll(f1, 32, 1)),
                jnp.where(lane < 64, pltpu.roll(f1, 64, 1), pltpu.roll(f2, 64, 1)),
                pltpu.roll(f2, 96, 1),
            ]
            for r in range(4):
                square[m, s, pl.ds(r, NC // 4, stride=4), :] = jnp.where(lane < NC, rows[r], 0.0)
            weights[m, s] = square[m, s].astype(jnp.bfloat16)

    for j in range(4):
        @pl.when(sources[j] != d)
        def _():
            arrived(j).wait_recv()

    answer = fields[APPLIES - 1]
    stride = d // 8

    def come(j):
        return pltpu.make_async_remote_copy(
            src_ref=answer.at[j], dst_ref=returned.at[stride],
            send_sem=back_send.at[j], recv_sem=back_recv.at[stride],
            device_id=(t, sources[j]), device_id_type=MESH,
        )

    def deliver(j):
        @pl.when(sources[j] != d)
        def _():
            come(j).start()

        @pl.when(sources[j] == d)
        def _():
            returned[stride] = answer[j]

    columns = [far_m - 1, near_m - 1, 2, 3, 4, 5]
    places = [[neighbours[c, 4 * d + s] % 4 for c in columns] for s in range(SITES)]
    sent = []
    for k in range(APPLIES):
        field = rhs if k == 0 else fields[k - 1]
        copies = []
        for i, ((to_t, to_d), _) in enumerate(sides):
            copies.append(
                pltpu.make_async_remote_copy(
                    src_ref=field, dst_ref=halos[6 * k + i],
                    send_sem=halo_send.at[k, i], recv_sem=halo_recv.at[k, i],
                    device_id=(to_t, to_d), device_id_type=MESH,
                )
            )
            copies[i].start()
        sent += copies
        halo = halos[6 * k : 6 * k + 6]
        totals = [
            product(s, (0, 5, 6), [field[s], field[places[s][4]], field[places[s][5]]])
            for s in range(SITES)
        ]
        for group in ((4, 5), (1, 2, 3), (0,)):
            for i in group:
                copies[i].wait_recv()
            for s in range(SITES):
                inputs = [halo[i][s] if i >= 4 else halo[i][places[s][i]] for i in group]
                totals[s] = totals[s] + product(s, [sides[i][1] for i in group], inputs)
        for s in range(SITES):
            new = rhs[s, :, :NC].astype(jnp.float32) - totals[s]
            fields[k][s, :, :NC] = new.astype(jnp.bfloat16)
            if k == APPLIES - 1:
                deliver(s)

    def came(s):
        return pltpu.make_async_remote_copy(
            src_ref=answer.at[s], dst_ref=returned.at[s],
            send_sem=back_send.at[s], recv_sem=back_recv.at[s],
            device_id=(t, d), device_id_type=MESH,
        )

    for s in range(4):
        @pl.when(dests[s] != d)
        def _():
            came(s).wait_recv()

    for a in range(SITES):
        back[a] = returned[strides[a]]
    for copy in sent:
        copy.wait_send()
    for s in range(4):
        @pl.when(dests[s] != d)
        def _():
            go(s).wait_send()
    for j in range(4):
        @pl.when(sources[j] != d)
        def _():
            come(j).wait_send()


def prolong(null, back, out_hbm, out, sems):
    stores = []
    for a in range(SITES):
        for c in range(KF // OUT_PIECE):
            part = pl.ds(c * OUT_PIECE, OUT_PIECE)
            out[a, :, part] = jnp.dot(
                back[a, :, :NC], null[a, :, part], preferred_element_type=jnp.float32
            ).astype(jnp.bfloat16)
            store = pltpu.make_async_copy(out.at[a, :, part], out_hbm.at[a, :, part], sems.at[a, c])
            store.start()
            stores.append(store)
    for store in stores:
        store.wait()


def body(fine_field, null_vectors, coarse_blocks, neighbours, owner_map):
    blocks = coarse_blocks[0].transpose(1, 0, 2)
    operands = (fine_field[0], null_vectors[0], blocks, neighbours.T, owner_map)
    hbm = pl.BlockSpec(memory_space=pl.ANY)
    field = pltpu.VMEM((SITES, NRHS, LANES), jnp.bfloat16)
    dma = pltpu.SemaphoreType.DMA
    vmem = pl.BlockSpec(memory_space=pltpu.VMEM)
    null, back = pl.pallas_call(
        kernel,
        out_shape=[
            pltpu.VMEM((SITES, NC, KF), jnp.bfloat16),
            pltpu.VMEM((SITES, NRHS, LANES), jnp.bfloat16),
        ],
        in_specs=[hbm] * 5,
        out_specs=[vmem, vmem],
        scratch_shapes=[
            pltpu.VMEM((SITES, NRHS, KF), jnp.bfloat16),
            pltpu.VMEM((9, SITES, NC * NC), jnp.bfloat16),
            pltpu.VMEM((9, 72 * 8, LANES), jnp.float32),
            pltpu.VMEM((9, SITES, NC, LANES), jnp.float32),
            pltpu.VMEM((9, SITES, NC, LANES), jnp.bfloat16),
            pltpu.SMEM((6, 128), jnp.int32),
            pltpu.SMEM((128,), jnp.int32),
            field, field, field,
            [field] * APPLIES,
            [field] * (6 * APPLIES),
            field,
            dma((2, SITES * CUTS)), dma((3,)),
            dma((4,)), dma((4,)),
            dma((APPLIES, 6)), dma((APPLIES, 6)),
            dma((4,)), dma((4,)),
        ],
        compiler_params=pltpu.CompilerParams(
            collective_id=0, has_side_effects=True, vmem_limit_bytes=48 * 1024 * 1024
        ),
    )(*[pltpu.with_memory_space_constraint(x, pltpu.HBM) for x in operands])
    result = pl.pallas_call(
        prolong,
        out_shape=jax.ShapeDtypeStruct((SITES, NRHS, KF), jnp.bfloat16),
        in_specs=[vmem, vmem],
        out_specs=hbm,
        scratch_shapes=[
            pltpu.VMEM((SITES, NRHS, KF), jnp.bfloat16),
            dma((SITES, KF // OUT_PIECE)),
        ],
        compiler_params=pltpu.CompilerParams(vmem_limit_bytes=16 * 1024 * 1024),
    )(*[pltpu.with_memory_space_constraint(x, pltpu.VMEM) for x in (null, back)])
    return result[None]


def solution(mesh):
    in_specs = (
        P("ta", "xyz", None, None),
        P("ta", "xyz", None, None),
        P("ta", "xyz", None, None),
        P(),
        P(),
    )
    out_specs = P("ta", "xyz", None, None)
    return jax.shard_map(body, mesh=mesh, in_specs=in_specs, out_specs=out_specs, check_vma=False)
```

```python
import jax
import jax.numpy as jnp
from jax import lax
from jax.experimental import pallas as pl
from jax.experimental.pallas import tpu as pltpu
from jax.sharding import PartitionSpec as P

MESH = pl.DeviceIdType.MESH
APPLIES = 3
SITES = 4
NRHS = 32
NC = 96
LANES = 128
KF = 6144
CUTS = 2
PIECE = KF // CUTS
OUT_PIECE = 2048
NT = (((1,), (1,)), ((), ()))


def dot_nt(a, b):
    return lax.dot_general(a, b, NT, preferred_element_type=jnp.float32)


def kernel(
    fine_hbm, null_hbm, blocks_hbm, neighbours_hbm, owner_hbm, null, back,
    fine, raw, spread, square, weights, neighbours, owner_map,
    rest, outgoing, rhs, fields, halos, returned,
    load_sem, table_sem, go_send, go_recv, halo_send, halo_recv, back_send, back_recv,
):
    t = lax.axis_index("ta")
    d = lax.axis_index("xyz")

    dests = [d // 4 + 8 * s for s in range(4)]
    sources = [4 * (d % 8) + j for j in range(4)]
    slot = d % 4
    across = (slot % 2) * 2 + slot // 2
    odd = across % 2
    far_at, near_at = (across + 3 + 2 * odd) % 4, (across + 1 + 2 * odd) % 4
    far = d - slot + (far_at % 2) * 2 + far_at // 2
    near = d - slot + (near_at % 2) * 2 + near_at // 2
    far_m, near_m = 2 - odd, 1 + odd
    y_up, y_down = (d + 4) % 32, (d + 28) % 32
    t_up, t_down = (t + 1) % 8, (t + 7) % 8
    sides = [
        ((t, far), far_m), ((t, near), near_m),
        ((t, y_down), 3), ((t, y_up), 4),
        ((t_down, d), 7), ((t_up, d), 8),
    ]

    barrier = pltpu.get_barrier_semaphore()
    for partner in sources:
        @pl.when(partner != d)
        def _():
            pl.semaphore_signal(barrier, inc=1, device_id=(t, partner), device_id_type=MESH)
    for (to_t, to_d), _ in sides:
        pl.semaphore_signal(barrier, inc=1, device_id=(to_t, to_d), device_id_type=MESH)

    loads = []
    for a in range(SITES):
        for c in range(CUTS):
            part = pl.ds(c * PIECE, PIECE)
            pair = [
                pltpu.make_async_copy(
                    fine_hbm.at[a, :, part], fine.at[a, :, part], load_sem.at[0, a * CUTS + c]
                ),
                pltpu.make_async_copy(
                    null_hbm.at[a, :, part], null.at[a, :, part], load_sem.at[1, a * CUTS + c]
                ),
            ]
            for copy in pair:
                copy.start()
            loads.append(pair)
    load_tables = [
        pltpu.make_async_copy(owner_hbm, owner_map, table_sem.at[0]),
        pltpu.make_async_copy(neighbours_hbm, neighbours, table_sem.at[1]),
        pltpu.make_async_copy(blocks_hbm, raw, table_sem.at[2]),
    ]
    for copy in load_tables:
        copy.start()

    for ref in [rest] + list(fields):
        ref[...] = jnp.zeros_like(ref)

    for a in range(SITES):
        total = jnp.zeros((NRHS, NC), jnp.float32)
        for c in range(CUTS):
            for copy in loads[a * CUTS + c]:
                copy.wait()
            part = pl.ds(c * PIECE, PIECE)
            total += dot_nt(fine[a, :, part], null[a, :, part])
        rest[a, :, :NC] = total.astype(jnp.bfloat16)

    load_tables[0].wait()
    load_tables[1].wait()
    columns = [far_m - 1, near_m - 1, 2, 3, 4, 5]
    places = [[neighbours[c, 4 * d + s] % 4 for c in columns] for s in range(SITES)]
    strides = [owner_map[4 * d + a] // 32 for a in range(SITES)]
    for s in range(4):
        chosen = 0
        for a in range(1, SITES):
            chosen = jnp.where(strides[a] == s, a, chosen)
        outgoing[s] = rest[chosen]

    own = 0
    for partner in dests:
        own = own + jnp.where(partner == d, 1, 0)
    pl.semaphore_wait(barrier, 6 + 4 - own)

    def go(s):
        return pltpu.make_async_remote_copy(
            src_ref=outgoing.at[s], dst_ref=rhs.at[slot],
            send_sem=go_send.at[s], recv_sem=go_recv.at[slot],
            device_id=(t, dests[s]), device_id_type=MESH,
        )

    def arrived(j):
        return pltpu.make_async_remote_copy(
            src_ref=outgoing.at[j], dst_ref=rhs.at[j],
            send_sem=go_send.at[j], recv_sem=go_recv.at[j],
            device_id=(t, d), device_id_type=MESH,
        )

    for s in range(4):
        @pl.when(dests[s] != d)
        def _():
            go(s).start()

        @pl.when(dests[s] == d)
        def _():
            rhs[slot] = outgoing[s]

    def product(s, ms, inputs):
        matrices = [weights[m, s] for m in ms]
        return dot_nt(jnp.concatenate(inputs, axis=1), jnp.concatenate(matrices, axis=1))

    load_tables[2].wait()
    lane = lax.broadcasted_iota(jnp.int32, (NC // 4, LANES), 1)

    @pl.loop(0, 9)
    def _(m):
        for j in range(72):
            spread[m, 8 * j : 8 * j + SITES, :] = raw[m, :, j * LANES : (j + 1) * LANES].astype(
                jnp.float32
            )
        for s in range(SITES):
            f0, f1, f2 = [spread[m, pl.ds(8 * j + s, NC // 4, stride=24), :] for j in range(3)]
            rows = [
                f0,
                jnp.where(lane < 32, pltpu.roll(f0, 32, 1), pltpu.roll(f1, 32, 1)),
                jnp.where(lane < 64, pltpu.roll(f1, 64, 1), pltpu.roll(f2, 64, 1)),
                pltpu.roll(f2, 96, 1),
            ]
            for r in range(4):
                square[m, s, pl.ds(r, NC // 4, stride=4), :] = jnp.where(lane < NC, rows[r], 0.0)
            weights[m, s] = square[m, s].astype(jnp.bfloat16)

    for j in range(4):
        @pl.when(sources[j] != d)
        def _():
            arrived(j).wait_recv()

    answer = fields[APPLIES - 1]
    stride = d // 8

    def come(j):
        return pltpu.make_async_remote_copy(
            src_ref=answer.at[j], dst_ref=returned.at[stride],
            send_sem=back_send.at[j], recv_sem=back_recv.at[stride],
            device_id=(t, sources[j]), device_id_type=MESH,
        )

    def deliver(j):
        @pl.when(sources[j] != d)
        def _():
            come(j).start()

        @pl.when(sources[j] == d)
        def _():
            returned[stride] = answer[j]

    sent = []
    for k in range(APPLIES):
        field = rhs if k == 0 else fields[k - 1]
        copies = []
        for i, ((to_t, to_d), _) in enumerate(sides):
            copies.append(
                pltpu.make_async_remote_copy(
                    src_ref=field, dst_ref=halos[6 * k + i],
                    send_sem=halo_send.at[k, i], recv_sem=halo_recv.at[k, i],
                    device_id=(to_t, to_d), device_id_type=MESH,
                )
            )
            copies[i].start()
        sent += copies
        halo = halos[6 * k : 6 * k + 6]
        totals = [
            product(s, (0, 5, 6), [field[s], field[places[s][4]], field[places[s][5]]])
            for s in range(SITES)
        ]
        for group in ((4, 5), (1, 2, 3), (0,)):
            for i in group:
                copies[i].wait_recv()
            for s in range(SITES):
                inputs = [halo[i][s] if i >= 4 else halo[i][places[s][i]] for i in group]
                totals[s] = totals[s] + product(s, [sides[i][1] for i in group], inputs)
        for s in range(SITES):
            new = rhs[s, :, :NC].astype(jnp.float32) - totals[s]
            fields[k][s, :, :NC] = new.astype(jnp.bfloat16)
            if k == APPLIES - 1:
                deliver(s)

    def came(s):
        return pltpu.make_async_remote_copy(
            src_ref=answer.at[s], dst_ref=returned.at[s],
            send_sem=back_send.at[s], recv_sem=back_recv.at[s],
            device_id=(t, d), device_id_type=MESH,
        )

    for copy in sent:
        copy.wait_send()
    for s in range(4):
        @pl.when(dests[s] != d)
        def _():
            go(s).wait_send()
    for j in range(4):
        @pl.when(sources[j] != d)
        def _():
            come(j).wait_send()

    for s in range(4):
        @pl.when(dests[s] != d)
        def _():
            came(s).wait_recv()

    for a in range(SITES):
        back[a] = returned[strides[a]]


def prolong(null, back, out_hbm, out, sems):
    stores = []
    for a in range(SITES):
        for c in range(KF // OUT_PIECE):
            part = pl.ds(c * OUT_PIECE, OUT_PIECE)
            out[a, :, part] = jnp.dot(
                back[a, :, :NC], null[a, :, part], preferred_element_type=jnp.float32
            ).astype(jnp.bfloat16)
            store = pltpu.make_async_copy(out.at[a, :, part], out_hbm.at[a, :, part], sems.at[a, c])
            store.start()
            stores.append(store)
    for store in stores:
        store.wait()


def body(fine_field, null_vectors, coarse_blocks, neighbours, owner_map):
    blocks = coarse_blocks[0].transpose(1, 0, 2)
    operands = (fine_field[0], null_vectors[0], blocks, neighbours.T, owner_map)
    hbm = pl.BlockSpec(memory_space=pl.ANY)
    field = pltpu.VMEM((SITES, NRHS, LANES), jnp.bfloat16)
    dma = pltpu.SemaphoreType.DMA
    vmem = pl.BlockSpec(memory_space=pltpu.VMEM)
    null, back = pl.pallas_call(
        kernel,
        out_shape=[
            pltpu.VMEM((SITES, NC, KF), jnp.bfloat16),
            pltpu.VMEM((SITES, NRHS, LANES), jnp.bfloat16),
        ],
        in_specs=[hbm] * 5,
        out_specs=[vmem, vmem],
        scratch_shapes=[
            pltpu.VMEM((SITES, NRHS, KF), jnp.bfloat16),
            pltpu.VMEM((9, SITES, NC * NC), jnp.bfloat16),
            pltpu.VMEM((9, 72 * 8, LANES), jnp.float32),
            pltpu.VMEM((9, SITES, NC, LANES), jnp.float32),
            pltpu.VMEM((9, SITES, NC, LANES), jnp.bfloat16),
            pltpu.SMEM((6, 128), jnp.int32),
            pltpu.SMEM((128,), jnp.int32),
            field, field, field,
            [field] * APPLIES,
            [field] * (6 * APPLIES),
            field,
            dma((2, SITES * CUTS)), dma((3,)),
            dma((4,)), dma((4,)),
            dma((APPLIES, 6)), dma((APPLIES, 6)),
            dma((4,)), dma((4,)),
        ],
        compiler_params=pltpu.CompilerParams(
            collective_id=0, has_side_effects=True, vmem_limit_bytes=48 * 1024 * 1024
        ),
    )(*[pltpu.with_memory_space_constraint(x, pltpu.HBM) for x in operands])
    result = pl.pallas_call(
        prolong,
        out_shape=jax.ShapeDtypeStruct((SITES, NRHS, KF), jnp.bfloat16),
        in_specs=[vmem, vmem],
        out_specs=hbm,
        scratch_shapes=[
            pltpu.VMEM((SITES, NRHS, KF), jnp.bfloat16),
            dma((SITES, KF // OUT_PIECE)),
        ],
        compiler_params=pltpu.CompilerParams(vmem_limit_bytes=16 * 1024 * 1024),
    )(*[pltpu.with_memory_space_constraint(x, pltpu.VMEM) for x in (null, back)])
    return result[None]


def solution(mesh):
    in_specs = (
        P("ta", "xyz", None, None),
        P("ta", "xyz", None, None),
        P("ta", "xyz", None, None),
        P(),
        P(),
    )
    out_specs = P("ta", "xyz", None, None)
    return jax.shard_map(body, mesh=mesh, in_specs=in_specs, out_specs=out_specs, check_vma=False)
```

```python
import jax
import jax.numpy as jnp
from jax import lax
from jax.experimental import pallas as pl
from jax.experimental.pallas import tpu as pltpu
from jax.sharding import PartitionSpec as P

MESH = pl.DeviceIdType.MESH
APPLIES = 3
SITES = 4
NRHS = 32
NC = 96
LANES = 128
KF = 6144
CUTS = 2
PIECE = KF // CUTS
OUT_PIECE = 2048
NT = (((1,), (1,)), ((), ()))


def dot_nt(a, b):
    return lax.dot_general(a, b, NT, preferred_element_type=jnp.float32)


def kernel(
    fine_hbm, null_hbm, blocks_hbm, neighbours_hbm, owner_hbm, null, back,
    fine, raw, spread, square, weights, neighbours, owner_map,
    rest, outgoing, rhs, fields, halos, returned,
    load_sem, table_sem, go_send, go_recv, halo_send, halo_recv, back_send, back_recv,
):
    t = lax.axis_index("ta")
    d = lax.axis_index("xyz")

    dests = [d // 4 + 8 * s for s in range(4)]
    sources = [4 * (d % 8) + j for j in range(4)]
    slot = d % 4
    across = (slot % 2) * 2 + slot // 2
    odd = across % 2
    far_at, near_at = (across + 3 + 2 * odd) % 4, (across + 1 + 2 * odd) % 4
    far = d - slot + (far_at % 2) * 2 + far_at // 2
    near = d - slot + (near_at % 2) * 2 + near_at // 2
    far_m, near_m = 2 - odd, 1 + odd
    y_up, y_down = (d + 4) % 32, (d + 28) % 32
    t_up, t_down = (t + 1) % 8, (t + 7) % 8
    sides = [
        ((t, far), far_m), ((t, near), near_m),
        ((t, y_down), 3), ((t, y_up), 4),
        ((t_down, d), 7), ((t_up, d), 8),
    ]

    barrier = pltpu.get_barrier_semaphore()
    for partner in sources:
        @pl.when(partner != d)
        def _():
            pl.semaphore_signal(barrier, inc=1, device_id=(t, partner), device_id_type=MESH)
    for (to_t, to_d), _ in sides:
        pl.semaphore_signal(barrier, inc=1, device_id=(to_t, to_d), device_id_type=MESH)

    loads = []
    for a in range(SITES):
        for c in range(CUTS):
            part = pl.ds(c * PIECE, PIECE)
            pair = [
                pltpu.make_async_copy(
                    fine_hbm.at[a, :, part], fine.at[a, :, part], load_sem.at[0, a * CUTS + c]
                ),
                pltpu.make_async_copy(
                    null_hbm.at[a, :, part], null.at[a, :, part], load_sem.at[1, a * CUTS + c]
                ),
            ]
            for copy in pair:
                copy.start()
            loads.append(pair)
    load_tables = [
        pltpu.make_async_copy(owner_hbm, owner_map, table_sem.at[0]),
        pltpu.make_async_copy(neighbours_hbm, neighbours, table_sem.at[1]),
        pltpu.make_async_copy(blocks_hbm, raw, table_sem.at[2]),
    ]
    for copy in load_tables:
        copy.start()

    for ref in [rest] + list(fields):
        ref[...] = jnp.zeros_like(ref)

    for a in range(SITES):
        total = jnp.zeros((NRHS, NC), jnp.float32)
        for c in range(CUTS):
            for copy in loads[a * CUTS + c]:
                copy.wait()
            part = pl.ds(c * PIECE, PIECE)
            total += dot_nt(fine[a, :, part], null[a, :, part])
        rest[a, :, :NC] = total.astype(jnp.bfloat16)

    load_tables[0].wait()
    load_tables[1].wait()
    columns = [far_m - 1, near_m - 1, 2, 3, 4, 5]
    places = [[neighbours[c, 4 * d + s] % 4 for c in columns] for s in range(SITES)]
    strides = [owner_map[4 * d + a] // 32 for a in range(SITES)]
    for s in range(4):
        chosen = 0
        for a in range(1, SITES):
            chosen = jnp.where(strides[a] == s, a, chosen)
        outgoing[s] = rest[chosen]

    own = 0
    for partner in dests:
        own = own + jnp.where(partner == d, 1, 0)
    pl.semaphore_wait(barrier, 6 + 4 - own)

    def go(s):
        return pltpu.make_async_remote_copy(
            src_ref=outgoing.at[s], dst_ref=rhs.at[slot],
            send_sem=go_send.at[s], recv_sem=go_recv.at[slot],
            device_id=(t, dests[s]), device_id_type=MESH,
        )

    def arrived(j):
        return pltpu.make_async_remote_copy(
            src_ref=outgoing.at[j], dst_ref=rhs.at[j],
            send_sem=go_send.at[j], recv_sem=go_recv.at[j],
            device_id=(t, d), device_id_type=MESH,
        )

    for s in range(4):
        @pl.when(dests[s] != d)
        def _():
            go(s).start()

        @pl.when(dests[s] == d)
        def _():
            rhs[slot] = outgoing[s]

    def product(s, ms, inputs):
        matrices = [weights[m, s] for m in ms]
        return dot_nt(jnp.concatenate(inputs, axis=1), jnp.concatenate(matrices, axis=1))

    load_tables[2].wait()
    lane = lax.broadcasted_iota(jnp.int32, (NC // 4, LANES), 1)

    @pl.loop(0, 9)
    def _(m):
        for j in range(72):
            spread[m, 8 * j : 8 * j + SITES, :] = raw[m, :, j * LANES : (j + 1) * LANES].astype(
                jnp.float32
            )
        for s in range(SITES):
            f0, f1, f2 = [spread[m, pl.ds(8 * j + s, NC // 4, stride=24), :] for j in range(3)]
            rows = [
                f0,
                jnp.where(lane < 32, pltpu.roll(f0, 32, 1), pltpu.roll(f1, 32, 1)),
                jnp.where(lane < 64, pltpu.roll(f1, 64, 1), pltpu.roll(f2, 64, 1)),
                pltpu.roll(f2, 96, 1),
            ]
            for r in range(4):
                square[m, s, pl.ds(r, NC // 4, stride=4), :] = jnp.where(lane < NC, rows[r], 0.0)
            weights[m, s] = square[m, s, :NC].astype(jnp.bfloat16)

    for j in range(4):
        @pl.when(sources[j] != d)
        def _():
            arrived(j).wait_recv()

    answer = fields[APPLIES - 1]
    stride = d // 8

    def come(j):
        return pltpu.make_async_remote_copy(
            src_ref=answer.at[j], dst_ref=returned.at[stride],
            send_sem=back_send.at[j], recv_sem=back_recv.at[stride],
            device_id=(t, sources[j]), device_id_type=MESH,
        )

    def deliver(j):
        @pl.when(sources[j] != d)
        def _():
            come(j).start()

        @pl.when(sources[j] == d)
        def _():
            returned[stride] = answer[j]

    sent = []
    for k in range(APPLIES):
        field = rhs if k == 0 else fields[k - 1]
        copies = []
        for i, ((to_t, to_d), _) in enumerate(sides):
            copies.append(
                pltpu.make_async_remote_copy(
                    src_ref=field, dst_ref=halos[6 * k + i],
                    send_sem=halo_send.at[k, i], recv_sem=halo_recv.at[k, i],
                    device_id=(to_t, to_d), device_id_type=MESH,
                )
            )
            copies[i].start()
        sent += copies
        halo = halos[6 * k : 6 * k + 6]
        totals = [
            product(s, (0, 5, 6), [field[s], field[places[s][4]], field[places[s][5]]])
            for s in range(SITES)
        ]
        for group in ((4, 5), (1, 2, 3), (0,)):
            for i in group:
                copies[i].wait_recv()
            for s in range(SITES):
                inputs = [halo[i][s] if i >= 4 else halo[i][places[s][i]] for i in group]
                totals[s] = totals[s] + product(s, [sides[i][1] for i in group], inputs)
        for s in range(SITES):
            new = rhs[s, :, :NC].astype(jnp.float32) - totals[s]
            fields[k][s, :, :NC] = new.astype(jnp.bfloat16)
            if k == APPLIES - 1:
                deliver(s)

    def came(s):
        return pltpu.make_async_remote_copy(
            src_ref=answer.at[s], dst_ref=returned.at[s],
            send_sem=back_send.at[s], recv_sem=back_recv.at[s],
            device_id=(t, d), device_id_type=MESH,
        )

    for copy in sent:
        copy.wait_send()
    for s in range(4):
        @pl.when(dests[s] != d)
        def _():
            go(s).wait_send()
    for j in range(4):
        @pl.when(sources[j] != d)
        def _():
            come(j).wait_send()

    for s in range(4):
        @pl.when(dests[s] != d)
        def _():
            came(s).wait_recv()

    for a in range(SITES):
        back[a] = returned[strides[a]]


def prolong(null, back, out_hbm, out, sems):
    stores = []
    for a in range(SITES):
        for c in range(KF // OUT_PIECE):
            part = pl.ds(c * OUT_PIECE, OUT_PIECE)
            out[a, :, part] = jnp.dot(
                back[a, :, :NC], null[a, :, part], preferred_element_type=jnp.float32
            ).astype(jnp.bfloat16)
            store = pltpu.make_async_copy(out.at[a, :, part], out_hbm.at[a, :, part], sems.at[a, c])
            store.start()
            stores.append(store)
    for store in stores:
        store.wait()


def body(fine_field, null_vectors, coarse_blocks, neighbours, owner_map):
    blocks = coarse_blocks[0].transpose(1, 0, 2)
    operands = (fine_field[0], null_vectors[0], blocks, neighbours.T, owner_map)
    hbm = pl.BlockSpec(memory_space=pl.ANY)
    field = pltpu.VMEM((SITES, NRHS, LANES), jnp.bfloat16)
    dma = pltpu.SemaphoreType.DMA
    vmem = pl.BlockSpec(memory_space=pltpu.VMEM)
    null, back = pl.pallas_call(
        kernel,
        out_shape=[
            pltpu.VMEM((SITES, NC, KF), jnp.bfloat16),
            pltpu.VMEM((SITES, NRHS, LANES), jnp.bfloat16),
        ],
        in_specs=[hbm] * 5,
        out_specs=[vmem, vmem],
        scratch_shapes=[
            pltpu.VMEM((SITES, NRHS, KF), jnp.bfloat16),
            pltpu.VMEM((9, SITES, NC * NC), jnp.bfloat16),
            pltpu.VMEM((9, 75 * 8, LANES), jnp.float32),
            pltpu.VMEM((9, SITES, NC + 8, LANES), jnp.float32),
            pltpu.VMEM((9, SITES, NC, LANES), jnp.bfloat16),
            pltpu.SMEM((6, 128), jnp.int32),
            pltpu.SMEM((128,), jnp.int32),
            field, field, field,
            [field] * APPLIES,
            [field] * (6 * APPLIES),
            field,
            dma((2, SITES * CUTS)), dma((3,)),
            dma((4,)), dma((4,)),
            dma((APPLIES, 6)), dma((APPLIES, 6)),
            dma((4,)), dma((4,)),
        ],
        compiler_params=pltpu.CompilerParams(
            collective_id=0, has_side_effects=True, vmem_limit_bytes=48 * 1024 * 1024
        ),
    )(*[pltpu.with_memory_space_constraint(x, pltpu.HBM) for x in operands])
    result = pl.pallas_call(
        prolong,
        out_shape=jax.ShapeDtypeStruct((SITES, NRHS, KF), jnp.bfloat16),
        in_specs=[vmem, vmem],
        out_specs=hbm,
        scratch_shapes=[
            pltpu.VMEM((SITES, NRHS, KF), jnp.bfloat16),
            dma((SITES, KF // OUT_PIECE)),
        ],
        compiler_params=pltpu.CompilerParams(vmem_limit_bytes=16 * 1024 * 1024),
    )(*[pltpu.with_memory_space_constraint(x, pltpu.VMEM) for x in (null, back)])
    return result[None]


def solution(mesh):
    in_specs = (
        P("ta", "xyz", None, None),
        P("ta", "xyz", None, None),
        P("ta", "xyz", None, None),
        P(),
        P(),
    )
    out_specs = P("ta", "xyz", None, None)
    return jax.shard_map(body, mesh=mesh, in_specs=in_specs, out_specs=out_specs, check_vma=False)
```

```python
import jax
import jax.numpy as jnp
from jax import lax
from jax.experimental import pallas as pl
from jax.experimental.pallas import tpu as pltpu
from jax.sharding import PartitionSpec as P

MESH = pl.DeviceIdType.MESH
APPLIES = 3
SITES = 4
NRHS = 32
NC = 96
LANES = 128
KF = 6144
CUTS = 2
PIECE = KF // CUTS
OUT_PIECE = 2048
NT = (((1,), (1,)), ((), ()))


def dot_nt(a, b):
    return lax.dot_general(a, b, NT, preferred_element_type=jnp.float32)


def kernel(
    fine_hbm, null_hbm, blocks_hbm, neighbours_hbm, owner_hbm, null, back,
    fine, raw, spread, square, weights, neighbours, owner_map,
    rest, outgoing, rhs, fields, halos, returned,
    far_raw, outward, returned_far,
    load_sem, table_sem, go_send, go_recv, halo_send, halo_recv, back_send, back_recv,
    far_send, far_recv, out_send, out_recv, first_send, first_recv,
):
    t = lax.axis_index("ta")
    d = lax.axis_index("xyz")

    dests = [d // 4 + 8 * s for s in range(4)]
    sources = [4 * (d % 8) + j for j in range(4)]
    slot = d % 4
    across = (slot % 2) * 2 + slot // 2
    odd = across % 2
    far_at, near_at = (across + 3 + 2 * odd) % 4, (across + 1 + 2 * odd) % 4
    far = d - slot + (far_at % 2) * 2 + far_at // 2
    near = d - slot + (near_at % 2) * 2 + near_at // 2
    far_m, near_m = 2 - odd, 1 + odd
    y_up, y_down = (d + 4) % 32, (d + 28) % 32
    t_up, t_down = (t + 1) % 8, (t + 7) % 8
    sides = [
        ((t, far), far_m), ((t, near), near_m),
        ((t, y_down), 3), ((t, y_up), 4),
        ((t_down, d), 7), ((t_up, d), 8),
    ]

    dest_fars = []
    for s in range(4):
        place = dests[s] % 4
        at = (place % 2) * 2 + place // 2
        at = (at + 3 + 2 * (at % 2)) % 4
        dest_fars.append(dests[s] - place + (at % 2) * 2 + at // 2)
    far_holders = [4 * (far % 8) + j for j in range(4)]

    barrier = pltpu.get_barrier_semaphore()
    for partner in sources + far_holders:
        @pl.when(partner != d)
        def _():
            pl.semaphore_signal(barrier, inc=1, device_id=(t, partner), device_id_type=MESH)
    for (to_t, to_d), _ in sides:
        pl.semaphore_signal(barrier, inc=1, device_id=(to_t, to_d), device_id_type=MESH)

    loads = []
    for a in range(SITES):
        for c in range(CUTS):
            part = pl.ds(c * PIECE, PIECE)
            pair = [
                pltpu.make_async_copy(
                    fine_hbm.at[a, :, part], fine.at[a, :, part], load_sem.at[0, a * CUTS + c]
                ),
                pltpu.make_async_copy(
                    null_hbm.at[a, :, part], null.at[a, :, part], load_sem.at[1, a * CUTS + c]
                ),
            ]
            for copy in pair:
                copy.start()
            loads.append(pair)
    load_tables = [
        pltpu.make_async_copy(owner_hbm, owner_map, table_sem.at[0]),
        pltpu.make_async_copy(neighbours_hbm, neighbours, table_sem.at[1]),
        pltpu.make_async_copy(blocks_hbm, raw, table_sem.at[2]),
    ]
    for copy in load_tables:
        copy.start()

    for ref in [rest, outward] + list(fields):
        ref[...] = jnp.zeros_like(ref)

    for a in range(SITES):
        total = jnp.zeros((NRHS, NC), jnp.float32)
        for c in range(CUTS):
            for copy in loads[a * CUTS + c]:
                copy.wait()
            part = pl.ds(c * PIECE, PIECE)
            total += dot_nt(fine[a, :, part], null[a, :, part])
        rest[a, :, :NC] = total.astype(jnp.bfloat16)

    load_tables[0].wait()
    load_tables[1].wait()
    strides = [owner_map[4 * d + a] // 32 for a in range(SITES)]
    for s in range(4):
        chosen = 0
        for a in range(1, SITES):
            chosen = jnp.where(strides[a] == s, a, chosen)
        outgoing[s] = rest[chosen]

    own = 0
    for partner in dests + dest_fars:
        own = own + jnp.where(partner == d, 1, 0)
    pl.semaphore_wait(barrier, 6 + 8 - own)

    def go(s):
        return pltpu.make_async_remote_copy(
            src_ref=outgoing.at[s], dst_ref=rhs.at[slot],
            send_sem=go_send.at[s], recv_sem=go_recv.at[slot],
            device_id=(t, dests[s]), device_id_type=MESH,
        )

    def arrived(j):
        return pltpu.make_async_remote_copy(
            src_ref=outgoing.at[j], dst_ref=rhs.at[j],
            send_sem=go_send.at[j], recv_sem=go_recv.at[j],
            device_id=(t, d), device_id_type=MESH,
        )

    for s in range(4):
        @pl.when(dests[s] != d)
        def _():
            go(s).start()

        @pl.when(dests[s] == d)
        def _():
            rhs[slot] = outgoing[s]

    def go_far(s):
        return pltpu.make_async_remote_copy(
            src_ref=outgoing.at[s], dst_ref=halos[0].at[slot],
            send_sem=first_send.at[s], recv_sem=first_recv.at[slot],
            device_id=(t, dest_fars[s]), device_id_type=MESH,
        )

    def arrived_far(j):
        return pltpu.make_async_remote_copy(
            src_ref=outgoing.at[j], dst_ref=halos[0].at[j],
            send_sem=first_send.at[j], recv_sem=first_recv.at[j],
            device_id=(t, d), device_id_type=MESH,
        )

    for s in range(4):
        @pl.when(dest_fars[s] != d)
        def _():
            go_far(s).start()

        @pl.when(dest_fars[s] == d)
        def _():
            halos[0][slot] = outgoing[s]

    far_blocks = pltpu.make_async_remote_copy(
        src_ref=blocks_hbm.at[far_m], dst_ref=far_raw,
        send_sem=far_send.at[0], recv_sem=far_recv.at[0],
        device_id=(t, far), device_id_type=MESH,
    )

    def product(s, ms, inputs):
        matrices = [weights[m, s] for m in ms]
        return dot_nt(jnp.concatenate(inputs, axis=1), jnp.concatenate(matrices, axis=1))

    load_tables[2].wait()
    lane = lax.broadcasted_iota(jnp.int32, (NC // 4, LANES), 1)

    def layout(m, source):
        for j in range(72):
            spread[m, 8 * j : 8 * j + SITES, :] = source[:, j * LANES : (j + 1) * LANES].astype(
                jnp.float32
            )
        for s in range(SITES):
            f0, f1, f2 = [spread[m, pl.ds(8 * j + s, NC // 4, stride=24), :] for j in range(3)]
            rows = [
                f0,
                jnp.where(lane < 32, pltpu.roll(f0, 32, 1), pltpu.roll(f1, 32, 1)),
                jnp.where(lane < 64, pltpu.roll(f1, 64, 1), pltpu.roll(f2, 64, 1)),
                pltpu.roll(f2, 96, 1),
            ]
            for r in range(4):
                square[m, s, pl.ds(r, NC // 4, stride=4), :] = jnp.where(lane < NC, rows[r], 0.0)
            weights[m, s] = square[m, s, :NC].astype(jnp.bfloat16)

    @pl.loop(0, 9)
    def _(m):
        layout(m, raw.at[m])

    for j in range(4):
        @pl.when(sources[j] != d)
        def _():
            arrived(j).wait_recv()

    answer = fields[2]
    stride = d // 8

    def come(j):
        return pltpu.make_async_remote_copy(
            src_ref=answer.at[j], dst_ref=returned.at[stride],
            send_sem=back_send.at[j], recv_sem=back_recv.at[stride],
            device_id=(t, sources[j]), device_id_type=MESH,
        )

    def deliver(j):
        @pl.when(sources[j] != d)
        def _():
            come(j).start()

        @pl.when(sources[j] == d)
        def _():
            returned[stride] = answer[j]


    def come_far(j):
        return pltpu.make_async_remote_copy(
            src_ref=outward.at[j], dst_ref=returned_far.at[stride],
            send_sem=out_send.at[j], recv_sem=out_recv.at[stride],
            device_id=(t, far_holders[j]), device_id_type=MESH,
        )

    def came_far(s):
        return pltpu.make_async_remote_copy(
            src_ref=outward.at[s], dst_ref=returned_far.at[s],
            send_sem=out_send.at[s], recv_sem=out_recv.at[s],
            device_id=(t, d), device_id_type=MESH,
        )

    columns = [far_m - 1, near_m - 1, 2, 3, 4, 5]
    places = [[neighbours[c, 4 * d + s] % 4 for c in columns] for s in range(SITES)]
    far_places = [neighbours[near_m - 1, 4 * far + s] % 4 for s in range(SITES)]
    sent = []

    def exchange(k, field, which):
        copies = {}
        for i in which:
            to_t, to_d = sides[i][0]
            copies[i] = pltpu.make_async_remote_copy(
                src_ref=field, dst_ref=halos[6 * k + i],
                send_sem=halo_send.at[k, i], recv_sem=halo_recv.at[k, i],
                device_id=(to_t, to_d), device_id_type=MESH,
            )
            copies[i].start()
            sent.append(copies[i])
        return copies

    def local(field):
        return [
            product(s, (0, 5, 6), [field[s], field[places[s][4]], field[places[s][5]]])
            for s in range(SITES)
        ]

    def arrive(k, copies, group, totals):
        for i in group:
            copies[i].wait_recv()
        halo = halos[6 * k : 6 * k + 6]
        for s in range(SITES):
            inputs = [halo[i][s] if i >= 4 else halo[i][places[s][i]] for i in group]
            totals[s] = totals[s] + product(s, [sides[i][1] for i in group], inputs)

    def right_side(s):
        return rhs[s, :, :NC].astype(jnp.float32)

    copies = exchange(0, rhs, range(1, 6))
    far_blocks.start()
    totals = local(rhs)
    for j in range(4):
        @pl.when(far_holders[j] != d)
        def _():
            arrived_far(j).wait_recv()
    for s in range(SITES):
        totals[s] = totals[s] + product(s, (far_m,), [halos[0][places[s][0]]])
    arrive(0, copies, (4, 5), totals)
    arrive(0, copies, (1, 2, 3), totals)
    for s in range(SITES):
        fields[0][s, :, :NC] = (right_side(s) - totals[s]).astype(jnp.bfloat16)

    copies = exchange(1, fields[0], range(6))
    totals = local(fields[0])
    far_blocks.wait_recv()
    layout(9, far_raw)
    arrive(1, copies, (4, 5), totals)
    arrive(1, copies, (1, 2, 3), totals)
    arrive(1, copies, (0,), totals)
    for s in range(SITES):
        fields[1][s, :, :NC] = (right_side(s) - totals[s]).astype(jnp.bfloat16)

    copies = exchange(2, fields[1], range(1, 6))
    for s in range(SITES):
        outward[s, :, :NC] = product(s, (9,), [fields[1][far_places[s]]]).astype(jnp.bfloat16)
    for j in range(4):
        @pl.when(far_holders[j] != d)
        def _():
            come_far(j).start()

        @pl.when(far_holders[j] == d)
        def _():
            returned_far[stride] = outward[j]
    totals = local(fields[1])
    arrive(2, copies, (4, 5), totals)
    arrive(2, copies, (1, 2, 3), totals)
    for s in range(SITES):
        fields[2][s, :, :NC] = (right_side(s) - totals[s]).astype(jnp.bfloat16)
        deliver(s)

    def came(s):
        return pltpu.make_async_remote_copy(
            src_ref=answer.at[s], dst_ref=returned.at[s],
            send_sem=back_send.at[s], recv_sem=back_recv.at[s],
            device_id=(t, d), device_id_type=MESH,
        )

    for s in range(4):
        @pl.when(dest_fars[s] != d)
        def _():
            came_far(s).wait_recv()
    for s in range(4):
        @pl.when(dests[s] != d)
        def _():
            came(s).wait_recv()

    for a in range(SITES):
        value = returned[strides[a]].astype(jnp.float32) - returned_far[strides[a]].astype(jnp.float32)
        back[a] = value.astype(jnp.bfloat16)
    for copy in sent:
        copy.wait_send()
    for s in range(4):
        @pl.when(dests[s] != d)
        def _():
            go(s).wait_send()

        @pl.when(dest_fars[s] != d)
        def _():
            go_far(s).wait_send()
    for j in range(4):
        @pl.when(sources[j] != d)
        def _():
            come(j).wait_send()

        @pl.when(far_holders[j] != d)
        def _():
            come_far(j).wait_send()
    far_blocks.wait_send()


def prolong(null, back, out_hbm, out, sems):
    stores = []
    for a in range(SITES):
        for c in range(KF // OUT_PIECE):
            part = pl.ds(c * OUT_PIECE, OUT_PIECE)
            out[a, :, part] = jnp.dot(
                back[a, :, :NC], null[a, :, part], preferred_element_type=jnp.float32
            ).astype(jnp.bfloat16)
            store = pltpu.make_async_copy(out.at[a, :, part], out_hbm.at[a, :, part], sems.at[a, c])
            store.start()
            stores.append(store)
    for store in stores:
        store.wait()


def body(fine_field, null_vectors, coarse_blocks, neighbours, owner_map):
    blocks = coarse_blocks[0].transpose(1, 0, 2)
    operands = (fine_field[0], null_vectors[0], blocks, neighbours.T, owner_map)
    hbm = pl.BlockSpec(memory_space=pl.ANY)
    field = pltpu.VMEM((SITES, NRHS, LANES), jnp.bfloat16)
    dma = pltpu.SemaphoreType.DMA
    vmem = pl.BlockSpec(memory_space=pltpu.VMEM)
    null, back = pl.pallas_call(
        kernel,
        out_shape=[
            pltpu.VMEM((SITES, NC, KF), jnp.bfloat16),
            pltpu.VMEM((SITES, NRHS, LANES), jnp.bfloat16),
        ],
        in_specs=[hbm] * 5,
        out_specs=[vmem, vmem],
        scratch_shapes=[
            pltpu.VMEM((SITES, NRHS, KF), jnp.bfloat16),
            pltpu.VMEM((9, SITES, NC * NC), jnp.bfloat16),
            pltpu.VMEM((10, 75 * 8, LANES), jnp.float32),
            pltpu.VMEM((10, SITES, NC + 8, LANES), jnp.float32),
            pltpu.VMEM((10, SITES, NC, LANES), jnp.bfloat16),
            pltpu.SMEM((6, 128), jnp.int32),
            pltpu.SMEM((128,), jnp.int32),
            field, field, field,
            [field] * APPLIES,
            [field] * (6 * APPLIES),
            field,
            pltpu.VMEM((SITES, NC * NC), jnp.bfloat16), field, field,
            dma((2, SITES * CUTS)), dma((3,)),
            dma((4,)), dma((4,)),
            dma((APPLIES, 6)), dma((APPLIES, 6)),
            dma((4,)), dma((4,)),
            dma((1,)), dma((1,)), dma((4,)), dma((4,)), dma((4,)), dma((4,)),
        ],
        compiler_params=pltpu.CompilerParams(
            collective_id=0, has_side_effects=True, vmem_limit_bytes=48 * 1024 * 1024
        ),
    )(*[pltpu.with_memory_space_constraint(x, pltpu.HBM) for x in operands])
    result = pl.pallas_call(
        prolong,
        out_shape=jax.ShapeDtypeStruct((SITES, NRHS, KF), jnp.bfloat16),
        in_specs=[vmem, vmem],
        out_specs=hbm,
        scratch_shapes=[
            pltpu.VMEM((SITES, NRHS, KF), jnp.bfloat16),
            dma((SITES, KF // OUT_PIECE)),
        ],
        compiler_params=pltpu.CompilerParams(vmem_limit_bytes=16 * 1024 * 1024),
    )(*[pltpu.with_memory_space_constraint(x, pltpu.VMEM) for x in (null, back)])
    return result[None]


def solution(mesh):
    in_specs = (
        P("ta", "xyz", None, None),
        P("ta", "xyz", None, None),
        P("ta", "xyz", None, None),
        P(),
        P(),
    )
    out_specs = P("ta", "xyz", None, None)
    return jax.shard_map(body, mesh=mesh, in_specs=in_specs, out_specs=out_specs, check_vma=False)
```

```python
import jax
import jax.numpy as jnp
from jax import lax
from jax.experimental import pallas as pl
from jax.experimental.pallas import tpu as pltpu
from jax.sharding import PartitionSpec as P

MESH = pl.DeviceIdType.MESH
APPLIES = 3
SITES = 4
NRHS = 32
NC = 96
LANES = 128
KF = 6144
CUTS = 2
PIECE = KF // CUTS
OUT_PIECE = 2048
NT = (((1,), (1,)), ((), ()))


def dot_nt(a, b):
    return lax.dot_general(a, b, NT, preferred_element_type=jnp.float32)


def kernel(
    fine_hbm, null_hbm, blocks_hbm, neighbours_hbm, owner_hbm, null, back,
    fine, raw, spread, square, weights, neighbours, owner_map,
    rest, outgoing, rhs, fields, halos, returned,
    far_raw, outward, returned_far,
    load_sem, table_sem, go_send, go_recv, halo_send, halo_recv, back_send, back_recv,
    far_send, far_recv, out_send, out_recv, first_send, first_recv,
):
    t = lax.axis_index("ta")
    d = lax.axis_index("xyz")

    dests = [d // 4 + 8 * s for s in range(4)]
    sources = [4 * (d % 8) + j for j in range(4)]
    slot = d % 4
    across = (slot % 2) * 2 + slot // 2
    odd = across % 2
    far_at, near_at = (across + 3 + 2 * odd) % 4, (across + 1 + 2 * odd) % 4
    far = d - slot + (far_at % 2) * 2 + far_at // 2
    near = d - slot + (near_at % 2) * 2 + near_at // 2
    far_m, near_m = 2 - odd, 1 + odd
    y_up, y_down = (d + 4) % 32, (d + 28) % 32
    t_up, t_down = (t + 1) % 8, (t + 7) % 8
    sides = [
        ((t, far), far_m), ((t, near), near_m),
        ((t, y_down), 3), ((t, y_up), 4),
        ((t_down, d), 7), ((t_up, d), 8),
    ]

    dest_fars = []
    for s in range(4):
        place = dests[s] % 4
        at = (place % 2) * 2 + place // 2
        at = (at + 3 + 2 * (at % 2)) % 4
        dest_fars.append(dests[s] - place + (at % 2) * 2 + at // 2)
    far_holders = [4 * (far % 8) + j for j in range(4)]

    barrier = pltpu.get_barrier_semaphore()
    for partner in sources + far_holders:
        @pl.when(partner != d)
        def _():
            pl.semaphore_signal(barrier, inc=1, device_id=(t, partner), device_id_type=MESH)
    for (to_t, to_d), _ in sides:
        pl.semaphore_signal(barrier, inc=1, device_id=(to_t, to_d), device_id_type=MESH)

    loads = []
    for a in range(SITES):
        for c in range(CUTS):
            part = pl.ds(c * PIECE, PIECE)
            pair = [
                pltpu.make_async_copy(
                    fine_hbm.at[a, :, part], fine.at[a, :, part], load_sem.at[0, a * CUTS + c]
                ),
                pltpu.make_async_copy(
                    null_hbm.at[a, :, part], null.at[a, :, part], load_sem.at[1, a * CUTS + c]
                ),
            ]
            for copy in pair:
                copy.start()
            loads.append(pair)
    load_tables = [
        pltpu.make_async_copy(owner_hbm, owner_map, table_sem.at[0]),
        pltpu.make_async_copy(neighbours_hbm, neighbours, table_sem.at[1]),
        pltpu.make_async_copy(blocks_hbm, raw, table_sem.at[2]),
    ]
    for copy in load_tables:
        copy.start()

    for ref in [rest, outward] + list(fields):
        ref[...] = jnp.zeros_like(ref)

    for a in range(SITES):
        total = jnp.zeros((NRHS, NC), jnp.float32)
        for c in range(CUTS):
            for copy in loads[a * CUTS + c]:
                copy.wait()
            part = pl.ds(c * PIECE, PIECE)
            total += dot_nt(fine[a, :, part], null[a, :, part])
        rest[a, :, :NC] = total.astype(jnp.bfloat16)

    load_tables[0].wait()
    load_tables[1].wait()
    strides = [owner_map[4 * d + a] // 32 for a in range(SITES)]
    for s in range(4):
        chosen = 0
        for a in range(1, SITES):
            chosen = jnp.where(strides[a] == s, a, chosen)
        outgoing[s] = rest[chosen]

    own = 0
    for partner in dests + dest_fars:
        own = own + jnp.where(partner == d, 1, 0)
    pl.semaphore_wait(barrier, 6 + 8 - own)

    def go(s):
        return pltpu.make_async_remote_copy(
            src_ref=outgoing.at[s], dst_ref=rhs.at[slot],
            send_sem=go_send.at[s], recv_sem=go_recv.at[slot],
            device_id=(t, dests[s]), device_id_type=MESH,
        )

    def arrived(j):
        return pltpu.make_async_remote_copy(
            src_ref=outgoing.at[j], dst_ref=rhs.at[j],
            send_sem=go_send.at[j], recv_sem=go_recv.at[j],
            device_id=(t, d), device_id_type=MESH,
        )

    for s in range(4):
        @pl.when(dests[s] != d)
        def _():
            go(s).start()

        @pl.when(dests[s] == d)
        def _():
            rhs[slot] = outgoing[s]

    def go_far(s):
        return pltpu.make_async_remote_copy(
            src_ref=outgoing.at[s], dst_ref=halos[0].at[slot],
            send_sem=first_send.at[s], recv_sem=first_recv.at[slot],
            device_id=(t, dest_fars[s]), device_id_type=MESH,
        )

    def arrived_far(j):
        return pltpu.make_async_remote_copy(
            src_ref=outgoing.at[j], dst_ref=halos[0].at[j],
            send_sem=first_send.at[j], recv_sem=first_recv.at[j],
            device_id=(t, d), device_id_type=MESH,
        )

    for s in range(4):
        @pl.when(dest_fars[s] != d)
        def _():
            go_far(s).start()

        @pl.when(dest_fars[s] == d)
        def _():
            halos[0][slot] = outgoing[s]

    far_blocks = pltpu.make_async_remote_copy(
        src_ref=blocks_hbm.at[far_m], dst_ref=far_raw,
        send_sem=far_send.at[0], recv_sem=far_recv.at[0],
        device_id=(t, far), device_id_type=MESH,
    )

    def product(s, ms, inputs):
        matrices = [weights[m, s] for m in ms]
        return dot_nt(jnp.concatenate(inputs, axis=1), jnp.concatenate(matrices, axis=1))

    load_tables[2].wait()
    lane = lax.broadcasted_iota(jnp.int32, (NC // 4, LANES), 1)

    def layout(m, source):
        for j in range(72):
            spread[m, 8 * j : 8 * j + SITES, :] = source[:, j * LANES : (j + 1) * LANES].astype(
                jnp.float32
            )
        for s in range(SITES):
            f0, f1, f2 = [spread[m, pl.ds(8 * j + s, NC // 4, stride=24), :] for j in range(3)]
            rows = [
                f0,
                jnp.where(lane < 32, pltpu.roll(f0, 32, 1), pltpu.roll(f1, 32, 1)),
                jnp.where(lane < 64, pltpu.roll(f1, 64, 1), pltpu.roll(f2, 64, 1)),
                pltpu.roll(f2, 96, 1),
            ]
            for r in range(4):
                square[m, s, pl.ds(r, NC // 4, stride=4), :] = jnp.where(lane < NC, rows[r], 0.0)
            weights[m, s] = square[m, s, :NC].astype(jnp.bfloat16)

    @pl.loop(0, 9)
    def _(m):
        layout(m, raw.at[m])

    for j in range(4):
        @pl.when(sources[j] != d)
        def _():
            arrived(j).wait_recv()

    answer = fields[2]
    stride = d // 8

    def come(j):
        return pltpu.make_async_remote_copy(
            src_ref=answer.at[j], dst_ref=returned.at[stride],
            send_sem=back_send.at[j], recv_sem=back_recv.at[stride],
            device_id=(t, sources[j]), device_id_type=MESH,
        )

    def deliver(j):
        @pl.when(sources[j] != d)
        def _():
            come(j).start()

        @pl.when(sources[j] == d)
        def _():
            returned[stride] = answer[j]


    def come_far(j):
        return pltpu.make_async_remote_copy(
            src_ref=outward.at[j], dst_ref=returned_far.at[stride],
            send_sem=out_send.at[j], recv_sem=out_recv.at[stride],
            device_id=(t, far_holders[j]), device_id_type=MESH,
        )

    def came_far(s):
        return pltpu.make_async_remote_copy(
            src_ref=outward.at[s], dst_ref=returned_far.at[s],
            send_sem=out_send.at[s], recv_sem=out_recv.at[s],
            device_id=(t, d), device_id_type=MESH,
        )

    columns = [far_m - 1, near_m - 1, 2, 3, 4, 5]
    places = [[neighbours[c, 4 * d + s] % 4 for c in columns] for s in range(SITES)]
    far_places = [neighbours[near_m - 1, 4 * far + s] % 4 for s in range(SITES)]
    sent = []

    def exchange(k, field, which):
        copies = {}
        for i in which:
            to_t, to_d = sides[i][0]
            copies[i] = pltpu.make_async_remote_copy(
                src_ref=field, dst_ref=halos[6 * k + i],
                send_sem=halo_send.at[k, i], recv_sem=halo_recv.at[k, i],
                device_id=(to_t, to_d), device_id_type=MESH,
            )
            copies[i].start()
            sent.append(copies[i])
        return copies

    def local(field):
        return [
            product(s, (0, 5, 6), [field[s], field[places[s][4]], field[places[s][5]]])
            for s in range(SITES)
        ]

    def arrive(k, copies, group, totals):
        for i in group:
            copies[i].wait_recv()
        halo = halos[6 * k : 6 * k + 6]
        for s in range(SITES):
            inputs = [halo[i][s] if i >= 4 else halo[i][places[s][i]] for i in group]
            totals[s] = totals[s] + product(s, [sides[i][1] for i in group], inputs)

    def right_side(s):
        return rhs[s, :, :NC].astype(jnp.float32)

    copies = exchange(0, rhs, range(1, 6))
    totals = local(rhs)
    for j in range(4):
        @pl.when(far_holders[j] != d)
        def _():
            arrived_far(j).wait_recv()
    for s in range(SITES):
        totals[s] = totals[s] + product(s, (far_m,), [halos[0][places[s][0]]])
    arrive(0, copies, (4, 5), totals)
    far_blocks.start()
    arrive(0, copies, (1, 2, 3), totals)
    for s in range(SITES):
        fields[0][s, :, :NC] = (right_side(s) - totals[s]).astype(jnp.bfloat16)

    copies = exchange(1, fields[0], range(6))
    totals = local(fields[0])
    far_blocks.wait_recv()
    layout(9, far_raw)
    arrive(1, copies, (4, 5), totals)
    arrive(1, copies, (1, 2, 3), totals)
    arrive(1, copies, (0,), totals)
    for s in range(SITES):
        fields[1][s, :, :NC] = (right_side(s) - totals[s]).astype(jnp.bfloat16)

    copies = exchange(2, fields[1], range(1, 6))
    for s in range(SITES):
        outward[s, :, :NC] = product(s, (9,), [fields[1][far_places[s]]]).astype(jnp.bfloat16)
    for j in range(4):
        @pl.when(far_holders[j] != d)
        def _():
            come_far(j).start()

        @pl.when(far_holders[j] == d)
        def _():
            returned_far[stride] = outward[j]
    totals = local(fields[1])
    arrive(2, copies, (4, 5), totals)
    arrive(2, copies, (1, 2, 3), totals)
    for s in range(SITES):
        fields[2][s, :, :NC] = (right_side(s) - totals[s]).astype(jnp.bfloat16)
        deliver(s)

    def came(s):
        return pltpu.make_async_remote_copy(
            src_ref=answer.at[s], dst_ref=returned.at[s],
            send_sem=back_send.at[s], recv_sem=back_recv.at[s],
            device_id=(t, d), device_id_type=MESH,
        )

    for s in range(4):
        @pl.when(dest_fars[s] != d)
        def _():
            came_far(s).wait_recv()
    for s in range(4):
        @pl.when(dests[s] != d)
        def _():
            came(s).wait_recv()

    for a in range(SITES):
        value = returned[strides[a]].astype(jnp.float32) - returned_far[strides[a]].astype(jnp.float32)
        back[a] = value.astype(jnp.bfloat16)
    for copy in sent:
        copy.wait_send()
    for s in range(4):
        @pl.when(dests[s] != d)
        def _():
            go(s).wait_send()

        @pl.when(dest_fars[s] != d)
        def _():
            go_far(s).wait_send()
    for j in range(4):
        @pl.when(sources[j] != d)
        def _():
            come(j).wait_send()

        @pl.when(far_holders[j] != d)
        def _():
            come_far(j).wait_send()
    far_blocks.wait_send()


def prolong(null, back, out_hbm, out, sems):
    stores = []
    for a in range(SITES):
        for c in range(KF // OUT_PIECE):
            part = pl.ds(c * OUT_PIECE, OUT_PIECE)
            out[a, :, part] = jnp.dot(
                back[a, :, :NC], null[a, :, part], preferred_element_type=jnp.float32
            ).astype(jnp.bfloat16)
            store = pltpu.make_async_copy(out.at[a, :, part], out_hbm.at[a, :, part], sems.at[a, c])
            store.start()
            stores.append(store)
    for store in stores:
        store.wait()


def body(fine_field, null_vectors, coarse_blocks, neighbours, owner_map):
    blocks = coarse_blocks[0].transpose(1, 0, 2)
    operands = (fine_field[0], null_vectors[0], blocks, neighbours.T, owner_map)
    hbm = pl.BlockSpec(memory_space=pl.ANY)
    field = pltpu.VMEM((SITES, NRHS, LANES), jnp.bfloat16)
    dma = pltpu.SemaphoreType.DMA
    vmem = pl.BlockSpec(memory_space=pltpu.VMEM)
    null, back = pl.pallas_call(
        kernel,
        out_shape=[
            pltpu.VMEM((SITES, NC, KF), jnp.bfloat16),
            pltpu.VMEM((SITES, NRHS, LANES), jnp.bfloat16),
        ],
        in_specs=[hbm] * 5,
        out_specs=[vmem, vmem],
        scratch_shapes=[
            pltpu.VMEM((SITES, NRHS, KF), jnp.bfloat16),
            pltpu.VMEM((9, SITES, NC * NC), jnp.bfloat16),
            pltpu.VMEM((10, 75 * 8, LANES), jnp.float32),
            pltpu.VMEM((10, SITES, NC + 8, LANES), jnp.float32),
            pltpu.VMEM((10, SITES, NC, LANES), jnp.bfloat16),
            pltpu.SMEM((6, 128), jnp.int32),
            pltpu.SMEM((128,), jnp.int32),
            field, field, field,
            [field] * APPLIES,
            [field] * (6 * APPLIES),
            field,
            pltpu.VMEM((SITES, NC * NC), jnp.bfloat16), field, field,
            dma((2, SITES * CUTS)), dma((3,)),
            dma((4,)), dma((4,)),
            dma((APPLIES, 6)), dma((APPLIES, 6)),
            dma((4,)), dma((4,)),
            dma((1,)), dma((1,)), dma((4,)), dma((4,)), dma((4,)), dma((4,)),
        ],
        compiler_params=pltpu.CompilerParams(
            collective_id=0, has_side_effects=True, vmem_limit_bytes=48 * 1024 * 1024
        ),
    )(*[pltpu.with_memory_space_constraint(x, pltpu.HBM) for x in operands])
    result = pl.pallas_call(
        prolong,
        out_shape=jax.ShapeDtypeStruct((SITES, NRHS, KF), jnp.bfloat16),
        in_specs=[vmem, vmem],
        out_specs=hbm,
        scratch_shapes=[
            pltpu.VMEM((SITES, NRHS, KF), jnp.bfloat16),
            dma((SITES, KF // OUT_PIECE)),
        ],
        compiler_params=pltpu.CompilerParams(vmem_limit_bytes=16 * 1024 * 1024),
    )(*[pltpu.with_memory_space_constraint(x, pltpu.VMEM) for x in (null, back)])
    return result[None]


def solution(mesh):
    in_specs = (
        P("ta", "xyz", None, None),
        P("ta", "xyz", None, None),
        P("ta", "xyz", None, None),
        P(),
        P(),
    )
    out_specs = P("ta", "xyz", None, None)
    return jax.shard_map(body, mesh=mesh, in_specs=in_specs, out_specs=out_specs, check_vma=False)
```

```python
import jax
import jax.numpy as jnp
from jax import lax
from jax.experimental import pallas as pl
from jax.experimental.pallas import tpu as pltpu
from jax.sharding import PartitionSpec as P

MESH = pl.DeviceIdType.MESH
APPLIES = 3
SITES = 4
NRHS = 32
NC = 96
LANES = 128
KF = 6144
CUTS = 2
PIECE = KF // CUTS
OUT_PIECE = 2048
NT = (((1,), (1,)), ((), ()))


def dot_nt(a, b):
    return lax.dot_general(a, b, NT, preferred_element_type=jnp.float32)


def kernel(
    fine_hbm, null_hbm, blocks_hbm, neighbours_hbm, owner_hbm, null, back,
    fine, raw, spread, square, weights, neighbours, owner_map,
    rest, outgoing, rhs, fields, halos, returned,
    far_raw, outward, returned_far,
    load_sem, table_sem, go_send, go_recv, halo_send, halo_recv, back_send, back_recv,
    far_send, far_recv, out_send, out_recv, first_send, first_recv,
):
    t = lax.axis_index("ta")
    d = lax.axis_index("xyz")

    dests = [d // 4 + 8 * s for s in range(4)]
    sources = [4 * (d % 8) + j for j in range(4)]
    slot = d % 4
    across = (slot % 2) * 2 + slot // 2
    odd = across % 2
    far_at, near_at = (across + 3 + 2 * odd) % 4, (across + 1 + 2 * odd) % 4
    far = d - slot + (far_at % 2) * 2 + far_at // 2
    near = d - slot + (near_at % 2) * 2 + near_at // 2
    far_m, near_m = 2 - odd, 1 + odd
    y_up, y_down = (d + 4) % 32, (d + 28) % 32
    t_up, t_down = (t + 1) % 8, (t + 7) % 8
    sides = [
        ((t, far), far_m), ((t, near), near_m),
        ((t, y_down), 3), ((t, y_up), 4),
        ((t_down, d), 7), ((t_up, d), 8),
    ]

    dest_fars = []
    for s in range(4):
        place = dests[s] % 4
        at = (place % 2) * 2 + place // 2
        at = (at + 3 + 2 * (at % 2)) % 4
        dest_fars.append(dests[s] - place + (at % 2) * 2 + at // 2)
    far_holders = [4 * (far % 8) + j for j in range(4)]

    barrier = pltpu.get_barrier_semaphore()
    for partner in sources + far_holders:
        @pl.when(partner != d)
        def _():
            pl.semaphore_signal(barrier, inc=1, device_id=(t, partner), device_id_type=MESH)
    for (to_t, to_d), _ in sides:
        pl.semaphore_signal(barrier, inc=1, device_id=(to_t, to_d), device_id_type=MESH)

    loads = []
    for a in range(SITES):
        for c in range(CUTS):
            part = pl.ds(c * PIECE, PIECE)
            pair = [
                pltpu.make_async_copy(
                    fine_hbm.at[a, :, part], fine.at[a, :, part], load_sem.at[0, a * CUTS + c]
                ),
                pltpu.make_async_copy(
                    null_hbm.at[a, :, part], null.at[a, :, part], load_sem.at[1, a * CUTS + c]
                ),
            ]
            for copy in pair:
                copy.start()
            loads.append(pair)
    load_tables = [
        pltpu.make_async_copy(owner_hbm, owner_map, table_sem.at[0]),
        pltpu.make_async_copy(neighbours_hbm, neighbours, table_sem.at[1]),
        pltpu.make_async_copy(blocks_hbm, raw, table_sem.at[2]),
    ]
    for copy in load_tables:
        copy.start()

    for ref in [rest, outward] + list(fields):
        ref[...] = jnp.zeros_like(ref)

    for a in range(SITES):
        total = jnp.zeros((NRHS, NC), jnp.float32)
        for c in range(CUTS):
            for copy in loads[a * CUTS + c]:
                copy.wait()
            part = pl.ds(c * PIECE, PIECE)
            total += dot_nt(fine[a, :, part], null[a, :, part])
        rest[a, :, :NC] = total.astype(jnp.bfloat16)

    load_tables[0].wait()
    load_tables[1].wait()
    strides = [owner_map[4 * d + a] // 32 for a in range(SITES)]
    for s in range(4):
        chosen = 0
        for a in range(1, SITES):
            chosen = jnp.where(strides[a] == s, a, chosen)
        outgoing[s] = rest[chosen]

    own = 0
    for partner in dests + dest_fars:
        own = own + jnp.where(partner == d, 1, 0)
    pl.semaphore_wait(barrier, 6 + 8 - own)

    def go(s):
        return pltpu.make_async_remote_copy(
            src_ref=outgoing.at[s], dst_ref=rhs.at[slot],
            send_sem=go_send.at[s], recv_sem=go_recv.at[slot],
            device_id=(t, dests[s]), device_id_type=MESH,
        )

    def arrived(j):
        return pltpu.make_async_remote_copy(
            src_ref=outgoing.at[j], dst_ref=rhs.at[j],
            send_sem=go_send.at[j], recv_sem=go_recv.at[j],
            device_id=(t, d), device_id_type=MESH,
        )

    for s in range(4):
        @pl.when(dests[s] != d)
        def _():
            go(s).start()

        @pl.when(dests[s] == d)
        def _():
            rhs[slot] = outgoing[s]

    def go_far(s):
        return pltpu.make_async_remote_copy(
            src_ref=outgoing.at[s], dst_ref=halos[0].at[slot],
            send_sem=first_send.at[s], recv_sem=first_recv.at[slot],
            device_id=(t, dest_fars[s]), device_id_type=MESH,
        )

    def arrived_far(j):
        return pltpu.make_async_remote_copy(
            src_ref=outgoing.at[j], dst_ref=halos[0].at[j],
            send_sem=first_send.at[j], recv_sem=first_recv.at[j],
            device_id=(t, d), device_id_type=MESH,
        )

    for s in range(4):
        @pl.when(dest_fars[s] != d)
        def _():
            go_far(s).start()

        @pl.when(dest_fars[s] == d)
        def _():
            halos[0][slot] = outgoing[s]

    far_blocks = pltpu.make_async_remote_copy(
        src_ref=blocks_hbm.at[far_m], dst_ref=far_raw,
        send_sem=far_send.at[0], recv_sem=far_recv.at[0],
        device_id=(t, far), device_id_type=MESH,
    )

    def product(s, ms, inputs):
        matrices = [weights[m, s] for m in ms]
        return dot_nt(jnp.concatenate(inputs, axis=1), jnp.concatenate(matrices, axis=1))

    load_tables[2].wait()
    lane = lax.broadcasted_iota(jnp.int32, (NC // 4, LANES), 1)

    def layout(m, source):
        for j in range(72):
            spread[m, 8 * j : 8 * j + SITES, :] = source[:, j * LANES : (j + 1) * LANES].astype(
                jnp.float32
            )
        for s in range(SITES):
            f0, f1, f2 = [spread[m, pl.ds(8 * j + s, NC // 4, stride=24), :] for j in range(3)]
            rows = [
                f0,
                jnp.where(lane < 32, pltpu.roll(f0, 32, 1), pltpu.roll(f1, 32, 1)),
                jnp.where(lane < 64, pltpu.roll(f1, 64, 1), pltpu.roll(f2, 64, 1)),
                pltpu.roll(f2, 96, 1),
            ]
            for r in range(4):
                square[m, s, pl.ds(r, NC // 4, stride=4), :] = jnp.where(lane < NC, rows[r], 0.0)
            weights[m, s] = square[m, s, :NC].astype(jnp.bfloat16)

    @pl.loop(0, 9)
    def _(m):
        layout(m, raw.at[m])

    for j in range(4):
        @pl.when(sources[j] != d)
        def _():
            arrived(j).wait_recv()

    answer = fields[2]
    stride = d // 8

    def come(j):
        return pltpu.make_async_remote_copy(
            src_ref=answer.at[j], dst_ref=returned.at[stride],
            send_sem=back_send.at[j], recv_sem=back_recv.at[stride],
            device_id=(t, sources[j]), device_id_type=MESH,
        )

    def deliver(j):
        @pl.when(sources[j] != d)
        def _():
            come(j).start()

        @pl.when(sources[j] == d)
        def _():
            returned[stride] = answer[j]


    def come_far(j):
        return pltpu.make_async_remote_copy(
            src_ref=outward.at[j], dst_ref=returned_far.at[stride],
            send_sem=out_send.at[j], recv_sem=out_recv.at[stride],
            device_id=(t, far_holders[j]), device_id_type=MESH,
        )

    def came_far(s):
        return pltpu.make_async_remote_copy(
            src_ref=outward.at[s], dst_ref=returned_far.at[s],
            send_sem=out_send.at[s], recv_sem=out_recv.at[s],
            device_id=(t, d), device_id_type=MESH,
        )

    columns = [far_m - 1, near_m - 1, 2, 3, 4, 5]
    places = [[neighbours[c, 4 * d + s] % 4 for c in columns] for s in range(SITES)]
    far_places = [neighbours[near_m - 1, 4 * far + s] % 4 for s in range(SITES)]
    sent = []

    def exchange(k, field, which):
        copies = {}
        for i in which:
            to_t, to_d = sides[i][0]
            copies[i] = pltpu.make_async_remote_copy(
                src_ref=field, dst_ref=halos[6 * k + i],
                send_sem=halo_send.at[k, i], recv_sem=halo_recv.at[k, i],
                device_id=(to_t, to_d), device_id_type=MESH,
            )
            copies[i].start()
            sent.append(copies[i])
        return copies

    def local(field):
        return [
            product(s, (0, 5, 6), [field[s], field[places[s][4]], field[places[s][5]]])
            for s in range(SITES)
        ]

    def arrive(k, copies, group, totals):
        for i in group:
            copies[i].wait_recv()
        halo = halos[6 * k : 6 * k + 6]
        for s in range(SITES):
            inputs = [halo[i][s] if i >= 4 else halo[i][places[s][i]] for i in group]
            totals[s] = totals[s] + product(s, [sides[i][1] for i in group], inputs)

    def right_side(s):
        return rhs[s, :, :NC].astype(jnp.float32)

    copies = exchange(0, rhs, range(1, 6))
    totals = local(rhs)
    far_blocks.start()
    for j in range(4):
        @pl.when(far_holders[j] != d)
        def _():
            arrived_far(j).wait_recv()
    for s in range(SITES):
        totals[s] = totals[s] + product(s, (far_m,), [halos[0][places[s][0]]])
    arrive(0, copies, (4, 5), totals)
    arrive(0, copies, (1, 2, 3), totals)
    for s in range(SITES):
        fields[0][s, :, :NC] = (right_side(s) - totals[s]).astype(jnp.bfloat16)

    copies = exchange(1, fields[0], range(6))
    totals = local(fields[0])
    far_blocks.wait_recv()
    layout(9, far_raw)
    arrive(1, copies, (4, 5), totals)
    arrive(1, copies, (1, 2, 3), totals)
    arrive(1, copies, (0,), totals)
    for s in range(SITES):
        fields[1][s, :, :NC] = (right_side(s) - totals[s]).astype(jnp.bfloat16)

    copies = exchange(2, fields[1], range(1, 6))
    for s in range(SITES):
        outward[s, :, :NC] = product(s, (9,), [fields[1][far_places[s]]]).astype(jnp.bfloat16)
    for j in range(4):
        @pl.when(far_holders[j] != d)
        def _():
            come_far(j).start()

        @pl.when(far_holders[j] == d)
        def _():
            returned_far[stride] = outward[j]
    totals = local(fields[1])
    arrive(2, copies, (4, 5), totals)
    arrive(2, copies, (1, 2, 3), totals)
    for s in range(SITES):
        fields[2][s, :, :NC] = (right_side(s) - totals[s]).astype(jnp.bfloat16)
        deliver(s)

    def came(s):
        return pltpu.make_async_remote_copy(
            src_ref=answer.at[s], dst_ref=returned.at[s],
            send_sem=back_send.at[s], recv_sem=back_recv.at[s],
            device_id=(t, d), device_id_type=MESH,
        )

    for s in range(4):
        @pl.when(dest_fars[s] != d)
        def _():
            came_far(s).wait_recv()
    for s in range(4):
        @pl.when(dests[s] != d)
        def _():
            came(s).wait_recv()

    for a in range(SITES):
        value = returned[strides[a]].astype(jnp.float32) - returned_far[strides[a]].astype(jnp.float32)
        back[a] = value.astype(jnp.bfloat16)
    for copy in sent:
        copy.wait_send()
    for s in range(4):
        @pl.when(dests[s] != d)
        def _():
            go(s).wait_send()

        @pl.when(dest_fars[s] != d)
        def _():
            go_far(s).wait_send()
    for j in range(4):
        @pl.when(sources[j] != d)
        def _():
            come(j).wait_send()

        @pl.when(far_holders[j] != d)
        def _():
            come_far(j).wait_send()
    far_blocks.wait_send()


def prolong(null, back, out_hbm, out, sems):
    stores = []
    for a in range(SITES):
        for c in range(KF // OUT_PIECE):
            part = pl.ds(c * OUT_PIECE, OUT_PIECE)
            out[a, :, part] = jnp.dot(
                back[a, :, :NC], null[a, :, part], preferred_element_type=jnp.float32
            ).astype(jnp.bfloat16)
            store = pltpu.make_async_copy(out.at[a, :, part], out_hbm.at[a, :, part], sems.at[a, c])
            store.start()
            stores.append(store)
    for store in stores:
        store.wait()


def body(fine_field, null_vectors, coarse_blocks, neighbours, owner_map):
    blocks = coarse_blocks[0].transpose(1, 0, 2)
    operands = (fine_field[0], null_vectors[0], blocks, neighbours.T, owner_map)
    hbm = pl.BlockSpec(memory_space=pl.ANY)
    field = pltpu.VMEM((SITES, NRHS, LANES), jnp.bfloat16)
    dma = pltpu.SemaphoreType.DMA
    vmem = pl.BlockSpec(memory_space=pltpu.VMEM)
    null, back = pl.pallas_call(
        kernel,
        out_shape=[
            pltpu.VMEM((SITES, NC, KF), jnp.bfloat16),
            pltpu.VMEM((SITES, NRHS, LANES), jnp.bfloat16),
        ],
        in_specs=[hbm] * 5,
        out_specs=[vmem, vmem],
        scratch_shapes=[
            pltpu.VMEM((SITES, NRHS, KF), jnp.bfloat16),
            pltpu.VMEM((9, SITES, NC * NC), jnp.bfloat16),
            pltpu.VMEM((10, 75 * 8, LANES), jnp.float32),
            pltpu.VMEM((10, SITES, NC + 8, LANES), jnp.float32),
            pltpu.VMEM((10, SITES, NC, LANES), jnp.bfloat16),
            pltpu.SMEM((6, 128), jnp.int32),
            pltpu.SMEM((128,), jnp.int32),
            field, field, field,
            [field] * APPLIES,
            [field] * (6 * APPLIES),
            field,
            pltpu.VMEM((SITES, NC * NC), jnp.bfloat16), field, field,
            dma((2, SITES * CUTS)), dma((3,)),
            dma((4,)), dma((4,)),
            dma((APPLIES, 6)), dma((APPLIES, 6)),
            dma((4,)), dma((4,)),
            dma((1,)), dma((1,)), dma((4,)), dma((4,)), dma((4,)), dma((4,)),
        ],
        compiler_params=pltpu.CompilerParams(
            collective_id=0, has_side_effects=True, vmem_limit_bytes=48 * 1024 * 1024
        ),
    )(*[pltpu.with_memory_space_constraint(x, pltpu.HBM) for x in operands])
    result = pl.pallas_call(
        prolong,
        out_shape=jax.ShapeDtypeStruct((SITES, NRHS, KF), jnp.bfloat16),
        in_specs=[vmem, vmem],
        out_specs=hbm,
        scratch_shapes=[
            pltpu.VMEM((SITES, NRHS, KF), jnp.bfloat16),
            dma((SITES, KF // OUT_PIECE)),
        ],
        compiler_params=pltpu.CompilerParams(vmem_limit_bytes=16 * 1024 * 1024),
    )(*[pltpu.with_memory_space_constraint(x, pltpu.VMEM) for x in (null, back)])
    return result[None]


def solution(mesh):
    in_specs = (
        P("ta", "xyz", None, None),
        P("ta", "xyz", None, None),
        P("ta", "xyz", None, None),
        P(),
        P(),
    )
    out_specs = P("ta", "xyz", None, None)
    return jax.shard_map(body, mesh=mesh, in_specs=in_specs, out_specs=out_specs, check_vma=False)
```
